32 devices in a mesh: groups: 2 (over y), vel: 4 (over z), cell: 2 (over x), sub: 2 (over core).
Axes of the slice: x: 2, y: 2, z: 4, core: 2. Of those that a mesh axis runs over, the one named last changes fastest.
Arguments:
- density: bfloat16 [768, 110592], P(('groups', 'cell', 'sub'), 'vel'), parts along dimension 0, may hold values from 0.5 to 1.5
- coder: bfloat16 [110592, 512], P('vel'), may hold values from -0.01953125 to 0.01953125
- w_latent: bfloat16 [512, 512], replicated, may hold values from -0.25 to 0.25
- b_latent: float32 [512], replicated, may hold values from -3 to 3
- restitution: float32 [768], P(('groups', 'cell', 'sub')), parts along dimension 0, may hold values from 0.3 to 0.95
- inflow: float32 [221184], P(('groups', 'vel')), parts along dimension 0, may hold values from 0.5 to 1.5
- flags: int32 [8], P('groups'), parts along dimension 0, may hold values from 0 to 1, as said below
- blocks: int32 [192], P(('groups', 'vel')), parts along dimension 0, may hold values from 0 to 95, each once
Outputs:
- density_out: bfloat16 [768, 110592], P(('groups', 'cell', 'sub'), 'vel'), parts along dimension 0
The draws below stay inside these ranges and needn't reach their ends.
There are 2 independent parts, one for each index of `groups`. The reference program is written for one: setup_inputs(seed, part) draws one part's arguments, and reference() takes and returns one part's arrays. A program takes and returns all parts, laid end to end along the dimension named above; an argument that names none is the same for every part. Nothing has to cross between parts.
Inputs may be any that keep to these rules, and one draw needn't show every extreme that they name: flags[b] = 1 joins block b of 96 cells to block b - 1 (block 0 to the last block); 0 makes that boundary an inflow boundary. Every draw holds both values. A permutation of the velocity blocks.
All inputs are finite; a program needn't handle non-finite values.
Results may differ from the reference program's by a relative error of at most 0.007.
Values may be sent and summed in bfloat16 or wider, within the bound.
A program may use at most 128 MiB of HBM per device.

```python
import math
import jax
import jax.numpy as jnp
import numpy as np
from jax import lax

VGRID = 48
LATENT = 512
VBLOCKS = 96
STEPS = 2
C_DEV = 96
VELS = 110592
BLOCKS = 4
CELLS = 384


def draw_flags(key, part):
    first, second, third = jax.random.split(jax.random.fold_in(key, 7), 3)
    base = (jax.random.randint(first, (BLOCKS,), 0, 4) > 0).astype(jnp.int32)
    closed = jax.random.randint(second, (), 0, BLOCKS)
    opened = (closed + 1 + jax.random.randint(third, (), 0, BLOCKS - 1)) % BLOCKS
    marks = jnp.arange(BLOCKS, dtype=jnp.int32)
    base = jnp.where(marks == closed, 0, base)
    base = jnp.where(marks == opened, 1, base)
    return base.astype(jnp.int32)


def level_of(key, extent, cuts, low, high):
    level = 1.0
    for position, shards_of in cuts:
        draws = jax.random.uniform(jax.random.fold_in(jax.random.fold_in(key, 6), position), (shards_of,), jnp.float32, low / len(cuts), high / len(cuts))
        level = level * jnp.repeat(jnp.exp(draws), extent[position] // shards_of).reshape((-1,) + (1,) * (len(extent) - 1 - position))
    return level


def centred(own_key, extent, scale, reach, cuts=(), held_as=jnp.bfloat16):
    array = scale * jax.random.normal(own_key, extent, jnp.float32)
    if cuts:
        array = array * level_of(own_key, extent, cuts, -0.22, 0.18)
    return jnp.clip(array, -reach, reach).astype(held_as)


def setup_inputs(seed: int = 0, part: int = 0) -> dict:
    arg_keys = jax.random.split(jax.random.key(seed), 9)
    own_keys = jax.random.split(jax.random.fold_in(arg_keys[8], part), 9)
    density = jnp.clip(0.5 + 1.0 * jax.random.uniform(own_keys[0], (CELLS, VELS), jnp.float32) ** level_of(own_keys[0], (CELLS, VELS), ((0, 4), (1, 4)), -0.2, 0.2), 0.5, 1.5).astype(jnp.bfloat16)
    coder = centred(arg_keys[1], (VELS, LATENT), VELS ** -0.5, 0.01953125, ((0, 4),))
    w_latent = centred(arg_keys[2], (LATENT, LATENT), LATENT ** -0.5, 0.25)
    b_latent = centred(arg_keys[3], (LATENT,), 0.5, 3.0, (), jnp.float32)
    restitution = jnp.clip(0.3 + 0.65 * jax.random.uniform(own_keys[4], (CELLS,), jnp.float32) ** level_of(own_keys[4], (CELLS,), ((0, 4),), -0.2, 0.2), 0.3, 0.95)
    inflow = jnp.clip(0.5 + 1.0 * jax.random.uniform(own_keys[5], (VELS,), jnp.float32) ** level_of(own_keys[5], (VELS,), ((0, 4),), -0.2, 0.2), 0.5, 1.5)
    flags = draw_flags(jax.random.fold_in(jax.random.fold_in(arg_keys[8], part), 71), part)
    blocks = jax.random.permutation(own_keys[7], VBLOCKS).astype(jnp.int32)
    return {"density": density, "coder": coder, "w_latent": w_latent, "b_latent": b_latent, "restitution": restitution, "inflow": inflow, "flags": flags, "blocks": blocks}


SINK_RATE = 0.5
COURANT = 0.9

def grid_moments():
    centres = (2.0 * np.arange(VGRID) + 1.0 - VGRID) / VGRID
    second = float(np.sum(centres ** 2))
    fourth = float(np.sum(centres ** 4))
    number = float(VGRID)
    total = number ** 3
    cross = 3.0 * number * number * second
    quartic = 3.0 * number * number * fourth + 6.0 * number * second * second
    square = number * number * second
    return (total, cross, quartic, square)

def component(number):
    return (2 * number + 1 - VGRID).astype(jnp.float32) / VGRID

def velocity_rows(blocks):
    width = VELS // VBLOCKS
    number = (blocks[:, None] * width + jnp.arange(width, dtype=jnp.int32)[None, :]).reshape(-1).astype(jnp.int32)
    along_x = component(number // (VGRID * VGRID))
    along_y = component(number // VGRID % VGRID)
    along_z = component(number % VGRID)
    kinetic = along_x * along_x + along_y * along_y + along_z * along_z
    return jnp.stack([jnp.ones_like(along_x), along_x, along_y, along_z, kinetic])

def advect(padded, courant):
    length = padded.shape[0] - 4
    magnitude = jnp.abs(courant)
    lower = padded[0:length + 1]
    centre = padded[1:length + 2]
    upper = padded[2:length + 3]
    beyond = padded[3:length + 4]
    upwind = (1.0 - magnitude) / 2.0
    curved = (1.0 - magnitude * magnitude) / 6.0
    forward = centre + upwind * (upper - centre) - curved * (upper - 2.0 * centre + lower)
    backward = upper + upwind * (centre - upper) - curved * (centre - 2.0 * upper + beyond)
    flux = courant * jnp.where(courant >= 0.0, forward, backward)
    return padded[2:length + 2] - (flux[1:] - flux[:-1])

def project(fstar, collision, moments, energy_sum, restitution, basis):
    total, cross, quartic, square = grid_moments()
    sink = -SINK_RATE * (1.0 - restitution * restitution) * energy_sum
    excess = moments[4] - sink
    determinant = total * quartic - cross * cross
    mass_mult = (quartic * moments[0] - cross * excess) / determinant
    energy_mult = (total * excess - cross * moments[0]) / determinant
    weights = jnp.stack([mass_mult, moments[1] / square, moments[2] / square, moments[3] / square, energy_mult])
    correction = lax.dot_general(weights, basis, (((0,), (0,)), ((), ())), precision=lax.Precision.HIGHEST)
    return fstar + (collision - correction)

def collide(fstar, coder, w_latent, b_latent, restitution, basis):
    coarse = fstar.astype(jnp.bfloat16)
    encoded = jnp.dot(coarse, coder, preferred_element_type=jnp.float32)
    energy_sum = jnp.dot(fstar, basis[4], precision=lax.Precision.HIGHEST)
    active = jnp.tanh(jnp.dot(encoded.astype(jnp.bfloat16), w_latent, preferred_element_type=jnp.float32) + b_latent).astype(jnp.bfloat16)
    collision = math.sqrt(VELS / LATENT) * lax.dot_general(active, coder, (((1,), (1,)), ((), ())), preferred_element_type=jnp.float32)
    moments = lax.dot_general(basis, collision, (((1,), (1,)), ((), ())), precision=lax.Precision.HIGHEST)
    return project(fstar, collision, moments, energy_sum, restitution, basis)

def reference(density, coder, w_latent, b_latent, restitution, inflow, flags, blocks):
    basis = velocity_rows(blocks)
    courant = COURANT * basis[1]
    block_count = CELLS // C_DEV
    state = density.astype(jnp.float32)
    open_left = (flags == 1)[:, None, None]
    open_right = (jnp.concatenate([flags[1:], flags[:1]]) == 1)[:, None, None]
    for section_index in range(STEPS):
        grouped = state.reshape(block_count, C_DEV, VELS)
        before = jnp.concatenate([grouped[-1:, -2:], grouped[:-1, -2:]], 0)
        after_rows = jnp.concatenate([grouped[1:, :2], grouped[:1, :2]], 0)
        before = jnp.where(open_left, before, inflow[None, None, :])
        after_rows = jnp.where(open_right, after_rows, inflow[None, None, :])

        def one_block(members):
            block_cells, lead_rows, tail_rows, restit_rows = members
            padded = jnp.concatenate([lead_rows, block_cells, tail_rows], 0)
            return collide(advect(padded, courant), coder, w_latent, b_latent, restit_rows, basis)
        state = lax.map(one_block, (grouped, before, after_rows, restitution.reshape(block_count, C_DEV))).reshape(CELLS, VELS)
    return state.astype(jnp.bfloat16)
```

```python
import functools
import math

import jax
import jax.numpy as jnp
import numpy as np
from jax import lax
from jax.experimental import pallas as pl
from jax.experimental.pallas import tpu as pltpu
from jax.sharding import PartitionSpec as P

VGRID = 48
VBLOCKS = 96
VELS = 110592
WIDTH = VELS // VBLOCKS
SINK_RATE = 0.5
COURANT = 0.9
PACK = 4
EXT = 16
FIRST = 4
MESH = pl.DeviceIdType.MESH
BF16, F32 = jnp.bfloat16, jnp.float32


def grid_moments():
    centres = (2.0 * np.arange(VGRID) + 1.0 - VGRID) / VGRID
    second = float(np.sum(centres**2))
    fourth = float(np.sum(centres**4))
    number = float(VGRID)
    total = number**3
    cross = 3.0 * number * number * second
    quartic = 3.0 * number * number * fourth + 6.0 * number * second * second
    square = number * number * second
    return (total, cross, quartic, square)


def offsets(cells, count):
    rows = np.full(cells + EXT, 10**6)
    rows[:cells] = np.arange(cells)
    rows[cells : cells + 4] = [-2, -1, cells, cells + 1]
    second = rows[None, :] - rows[:cells, None]
    second = np.where(rows[None, :] > 10**5, 9, second)
    first = []
    for number in range(count):
        cols = np.full(cells + 2 * EXT, 10**7)
        cols[:cells] = np.arange(cells)
        at = cells + 4 * (number % PACK)
        cols[at : at + 4] = np.arange(-4, 0)
        cols[at + EXT : at + EXT + 4] = cells + np.arange(4)
        first.append(cols[None, :] - rows[:, None])
    first = np.stack(first)
    clean = lambda table: np.where(np.abs(table) <= 2, table, 9).astype(np.int32)
    return clean(first), clean(second)[None]


def stencil(courant, table):
    a = jnp.abs(courant)
    u = (1.0 - a) / 2.0
    q = (1.0 - a * a) / 6.0
    near = a * (1.0 - u + 3.0 * q)
    far = -a * q
    ahead = -a * (u - q)
    here = 1.0 - a * (1.0 - 2.0 * u + 3.0 * q)
    up = courant >= 0.0
    zero = jnp.zeros_like(a)
    weights = {
        -2: jnp.where(up, far, zero),
        -1: jnp.where(up, near, ahead),
        0: here,
        1: jnp.where(up, ahead, near),
        2: jnp.where(up, zero, far),
    }
    table = jnp.asarray(table)
    full = sum(jnp.where(table == o, w[:, None, None], 0.0) for o, w in weights.items())
    high = full.astype(BF16)
    low = (full - high.astype(F32)).astype(BF16)
    return jnp.concatenate([high, low], axis=2)


def dot(a, b):
    return jnp.dot(a, b, preferred_element_type=F32)


def dot_t(a, b, **kw):
    return lax.dot_general(a, b, (((1,), (1,)), ((), ())), preferred_element_type=F32, **kw)


def kernel(
    n, owners, cells, scale,
    coder_hbm, dens_hbm, left_ref, right_ref, basis_ref, a1_ref, a2_ref, energy_ref, inflow_ref,
    keep_ref, w_ref, bias_ref, rest_ref,
    out_hbm,
    coder_v, p_v, f_v, acc, eacc, send, recv, part, gath, esend, erecv, bsend, brecv, bgath, mult, act_v,
    coder_sem, dens_sem, out_sem, s_send, s_recv, g_send, g_recv, e_send, e_recv, b_send, b_recv, c_send, c_recv,
):
    me = lax.axis_index("vel")
    count = coder_v.shape[0]
    rows = cells + EXT
    latent = coder_v.shape[2]
    piece = latent // owners

    def coder_copy(b):
        return pltpu.make_async_copy(coder_hbm.at[b], coder_v.at[b], coder_sem.at[b])

    def columns(b):
        return pl.ds(pl.multiple_of(b * WIDTH, 128), WIDTH)

    def dens_copy(b):
        return pltpu.make_async_copy(dens_hbm.at[:, columns(b)], p_v.at[b], dens_sem.at[b])

    def out_copy(b):
        return pltpu.make_async_copy(p_v.at[b], out_hbm.at[:, columns(b)], out_sem.at[b])

    @pl.loop(0, count)
    def _(b):
        dens_copy(b).start()
        coder_copy(b).start()

    barrier = pltpu.get_barrier_semaphore()
    for d in range(1, n):
        pl.semaphore_signal(
            barrier, inc=1, device_id={"vel": lax.rem(me + d, n)}, device_id_type=MESH
        )
    pl.semaphore_wait(barrier, n - 1)

    def only(test, run):
        if n == owners:
            run()
        else:
            pl.when(test)(run)

    def energy_of(f, b):
        e = energy_ref[b]
        total = f[:, :128] * e[:, :128]
        for g in range(128, WIDTH, 128):
            total += f[:, g : g + 128] * e[:, g : g + 128]
        return total

    def exchange(step, size):
        col = jnp.sum(eacc[:size], axis=1, keepdims=True)
        eye = lax.broadcasted_iota(jnp.int32, (size, 128), 0) == lax.broadcasted_iota(
            jnp.int32, (size, 128), 1
        )
        row = jnp.sum(jnp.where(eye, col, 0.0), axis=0, keepdims=True)
        esend[step] = jnp.broadcast_to(row, (8, 128))
        for q in range(owners):
            value = acc[:size, q * piece : (q + 1) * piece]
            part[q, :size] = value
            send[step, q, :size] = value.astype(BF16)
            if step == 0:
                bsend[q] = acc[cells:rows, q * piece : (q + 1) * piece]

        def remote(src, dst, ss, rs, d):
            return pltpu.make_async_remote_copy(
                src_ref=src, dst_ref=dst, send_sem=ss, recv_sem=rs,
                device_id={"vel": lax.rem(me + d, n)}, device_id_type=MESH,
            )

        def scatter(d):
            to = lax.rem(me + d, n)
            made = [
                remote(
                    send.at[step, to, pl.ds(0, size)], recv.at[step, d - 1, pl.ds(0, size)],
                    s_send.at[step, d - 1], s_recv.at[step, d - 1], d,
                )
            ]
            if step == 0:
                made.append(
                    remote(bsend.at[to], brecv.at[d - 1], b_send.at[d - 1], b_recv.at[d - 1], d)
                )
            return made

        def spread(d):
            made = [
                remote(
                    gath.at[step, me, pl.ds(0, size)], gath.at[step, me, pl.ds(0, size)],
                    g_send.at[step, d - 1], g_recv.at[step, me], d,
                )
            ]
            if step == 0:
                made.append(
                    remote(bgath.at[me], bgath.at[me], c_send.at[d - 1], c_recv.at[me], d)
                )
            return made

        def arrival(owner):
            made = [
                remote(
                    gath.at[step, owner, pl.ds(0, size)], gath.at[step, owner, pl.ds(0, size)],
                    g_send.at[step, 0], g_recv.at[step, owner], 1,
                )
            ]
            if step == 0:
                made.append(
                    remote(bgath.at[owner], bgath.at[owner], c_send.at[0], c_recv.at[owner], 1)
                )
            return made

        def tell(d):
            return remote(
                esend.at[step], erecv.at[step, d - 1], e_send.at[step, d - 1], e_recv.at[step, d - 1], d
            )

        for d in range(1, n):
            only(lax.rem(me + d, n) < owners, lambda d=d: [c.start() for c in scatter(d)] and None)
        for d in range(1, n):
            tell(d).start()

        def reduce():
            total = part[me, :size]
            for d in range(1, n):
                for c in scatter(d):
                    c.wait_recv()
                total += recv[step, d - 1, :size].astype(F32)
            gath[step, me, :size] = total.astype(BF16)
            if step == 0:
                base = bsend[me]
                for d in range(1, n):
                    base += brecv[d - 1]
                bgath[me] = base
            for d in range(1, n):
                for c in spread(d):
                    c.start()

        only(me < owners, reduce)
        for d in range(1, n):
            only(lax.rem(me + d, n) < owners, lambda d=d: [c.wait_send() for c in scatter(d)] and None)
        for d in range(1, n):
            tell(d).wait()
        only(me < owners, lambda: [c.wait_send() for d in range(1, n) for c in spread(d)] and None)
        for d in range(1, n):
            owner = lax.rem(me + d, n)
            only(owner < owners, lambda owner=owner: [c.wait_recv() for c in arrival(owner)] and None)
        row = esend[step]
        for d in range(1, n):
            row += erecv[step, d - 1]
        return jnp.sum(jnp.where(eye, row[:1], 0.0), axis=1, keepdims=True)

    def latent_layer(step, size):
        energy_sum = exchange(step, size)
        encoded = jnp.concatenate([gath[step, q, :size] for q in range(owners)], axis=1)
        active = jnp.tanh(dot(encoded, w_ref[...]) + bias_ref[...]).astype(BF16)
        act_v[:size] = active
        base = jnp.concatenate([bgath[q] for q in range(owners)], axis=1)
        sums = scale * dot_t(active.astype(F32), base, precision=lax.Precision.HIGHEST)
        total, cross, quartic, square = grid_moments()
        sink = -SINK_RATE * (1.0 - rest_ref[:size] * rest_ref[:size]) * energy_sum
        grid = float(VGRID)
        m = [sums[:, FIRST + i : FIRST + i + 1] for i in range(6)]
        excess = (m[4] + m[5]) / (grid * grid) - sink
        determinant = total * quartic - cross * cross
        mass_mult = (quartic * m[0] - cross * excess) / determinant
        energy_mult = (total * excess - cross * m[0]) / determinant / (grid * grid)
        values = [mass_mult] + [m[i] / (square * grid * grid) for i in (1, 2, 3)] + [energy_mult] * 2
        lane = lax.broadcasted_iota(jnp.int32, (size, 2 * EXT), 1)
        full = jnp.zeros((size, 2 * EXT), F32)
        for i, value in enumerate(values):
            full = jnp.where(lane % EXT == FIRST + i, -value, full)
        high = full.astype(BF16).astype(F32)
        mult[:size] = jnp.where(lane < EXT, high, full - high).astype(BF16)

    def advanced(b, size):
        base = basis_ref[b]
        collision = dot_t(act_v[:size], coder_v[b])
        correction = dot(mult[:size], jnp.concatenate([base, base], axis=0))
        return (f_v[b, :size] + correction + scale * collision).astype(BF16)

    acc[...] = jnp.zeros_like(acc)
    eacc[...] = jnp.zeros_like(eacc)
    extra = lax.broadcasted_iota(jnp.int32, (EXT, WIDTH), 0) >= FIRST

    @pl.loop(0, count)
    def _(b):
        dens_copy(b).wait()
        x = jnp.concatenate([p_v[b], left_ref[b // PACK], right_ref[b // PACK]], axis=0)
        f = dot(a1_ref[b], jnp.concatenate([x, x], axis=0))
        f_v[b] = f
        eacc[...] += energy_of(f, b)
        coarse = f.astype(BF16)
        tail = jnp.where(extra, basis_ref[b].astype(F32), f[cells:]).astype(BF16)
        coder_copy(b).wait()
        acc[...] += dot(jnp.concatenate([coarse[:cells], tail], axis=0), coder_v[b])

    latent_layer(0, rows)
    acc[...] = jnp.zeros_like(acc)
    eacc[...] = jnp.zeros_like(eacc)

    @pl.loop(0, count)
    def _(b):
        state = advanced(b, rows)
        edge = jnp.where(keep_ref[...] > 0.0, state[cells:].astype(F32), inflow_ref[b]).astype(BF16)
        x = jnp.concatenate([state[:cells], edge], axis=0)
        f = dot(a2_ref[b], jnp.concatenate([x, x], axis=0))
        f_v[b, :cells] = f
        eacc[:cells] += energy_of(f, b)
        acc[:cells] += dot(f.astype(BF16), coder_v[b])

    latent_layer(1, cells)

    @pl.loop(0, count)
    def _(b):
        p_v[b] = advanced(b, cells)
        out_copy(b).start()

    @pl.loop(0, count)
    def _(b):
        out_copy(b).wait()


def ring(value, step):
    count = lax.axis_size("cell") * lax.axis_size("sub")
    return lax.ppermute(value, ("cell", "sub"), [(i, (i + step) % count) for i in range(count)])


def body(density, coder, w_latent, b_latent, restitution, inflow, flags, blocks):
    cells, columns = density.shape
    latent = coder.shape[1]
    count = columns // WIDTH
    chunks = -(-count // PACK)
    n = lax.axis_size("vel")
    owners = min(n, latent // 128)
    rows = cells + EXT

    left = ring(density[-4:], 1)
    right = ring(density[:4], -1)
    rest_left = ring(restitution[-2:], 1)
    rest_right = ring(restitution[:2], -1)

    sub_count = lax.axis_size("sub")
    position = lax.axis_index("cell") * sub_count + lax.axis_index("sub")
    block_count = lax.axis_size("cell") * sub_count
    open_left = lax.dynamic_index_in_dim(flags, position, 0, keepdims=False) == 1
    open_right = (
        lax.dynamic_index_in_dim(flags, (position + 1) % block_count, 0, keepdims=False) == 1
    )

    number = blocks[:, None] * WIDTH + jnp.arange(WIDTH, dtype=jnp.int32)[None, :]
    nx = 2 * (number // (VGRID * VGRID)) + 1 - VGRID
    ny = 2 * (number // VGRID % VGRID) + 1 - VGRID
    nz = 2 * (number % VGRID) + 1 - VGRID
    kinetic = nx * nx + ny * ny + nz * nz
    upper = kinetic // 64 * 64
    zero = jnp.zeros_like(nx)
    basis = jnp.stack(
        [zero] * FIRST + [zero + 1, nx, ny, nz, upper, kinetic - upper] + [zero] * (EXT - FIRST - 6),
        axis=1,
    ).astype(BF16)
    energy = (kinetic.astype(F32) / (VGRID * VGRID))[:, None, :]
    along = 2 * (blocks * WIDTH // (VGRID * VGRID)) + 1 - VGRID
    courant = COURANT * (along.astype(F32) / VGRID)
    first, second = offsets(cells, count)
    a1 = stencil(courant, first)
    a2 = stencil(courant, second)

    def packed(ghosts, is_open):
        ghosts = jnp.where(is_open, ghosts, inflow.astype(BF16)[None])
        ghosts = ghosts.reshape(4, count, WIDTH).transpose(1, 0, 2)
        ghosts = jnp.pad(ghosts, ((0, chunks * PACK - count), (0, 0), (0, 0)))
        return ghosts.reshape(chunks, PACK * 4, WIDTH)

    rest = jnp.concatenate([restitution, rest_left, rest_right, jnp.zeros((EXT - 4,), F32)])
    side = jnp.arange(EXT)
    keep = jnp.where(side < 2, open_left, jnp.where(side < 4, open_right, True)).astype(F32)

    vmem = pl.BlockSpec(memory_space=pltpu.VMEM)
    hbm = pl.BlockSpec(memory_space=pl.ANY)
    dma = pltpu.SemaphoreType.DMA
    piece = latent // owners
    others = max(n - 1, 1)
    flops = 2 * columns * latent * (4 * rows) + 2 * columns * 512 * rows
    return pl.pallas_call(
        functools.partial(kernel, n, owners, cells, math.sqrt(VELS / latent)),
        out_shape=jax.ShapeDtypeStruct((cells, columns), BF16),
        in_specs=[hbm, hbm] + [vmem] * 11,
        out_specs=hbm,
        scratch_shapes=[
            pltpu.VMEM((count, WIDTH, latent), BF16),
            pltpu.VMEM((count, cells, WIDTH), BF16),
            pltpu.VMEM((count, rows, WIDTH), F32),
            pltpu.VMEM((rows, latent), F32),
            pltpu.VMEM((rows, 128), F32),
            pltpu.VMEM((2, owners, rows, piece), BF16),
            pltpu.VMEM((2, others, rows, piece), BF16),
            pltpu.VMEM((owners, rows, piece), F32),
            pltpu.VMEM((2, owners, rows, piece), BF16),
            pltpu.VMEM((2, 8, 128), F32),
            pltpu.VMEM((2, others, 8, 128), F32),
            pltpu.VMEM((owners, EXT, piece), F32),
            pltpu.VMEM((others, EXT, piece), F32),
            pltpu.VMEM((owners, EXT, piece), F32),
            pltpu.VMEM((rows, 2 * EXT), BF16),
            pltpu.VMEM((rows, latent), BF16),
            dma((count,)), dma((count,)), dma((count,)),
            dma((2, others)), dma((2, others)), dma((2, others)), dma((2, owners)),
            dma((2, others)), dma((2, others)),
            dma((others,)), dma((others,)), dma((others,)), dma((owners,)),
        ],
        compiler_params=pltpu.CompilerParams(
            collective_id=0, has_side_effects=True, vmem_limit_bytes=60 * 1024 * 1024
        ),
        cost_estimate=pl.CostEstimate(
            flops=flops, bytes_accessed=2 * columns * (latent + 2 * cells), transcendentals=0
        ),
    )(
        coder.reshape(count, WIDTH, latent), density,
        packed(left, open_left), packed(right, open_right), basis, a1, a2, energy,
        inflow.reshape(count, 1, WIDTH), keep[:, None], w_latent, b_latent[None, :], rest[:, None],
    )


def solution(mesh):
    return jax.shard_map(
        body,
        mesh=mesh,
        in_specs=(
            P(("groups", "cell", "sub"), "vel"),
            P("vel", None),
            P(),
            P(),
            P(("groups", "cell", "sub")),
            P(("groups", "vel")),
            P("groups"),
            P(("groups", "vel")),
        ),
        out_specs=P(("groups", "cell", "sub"), "vel"),
        check_vma=False,
    )
```

```python
import functools
import math

import jax
import jax.numpy as jnp
import numpy as np
from jax import lax
from jax.experimental import pallas as pl
from jax.experimental.pallas import tpu as pltpu
from jax.sharding import PartitionSpec as P

VGRID = 48
VBLOCKS = 96
VELS = 110592
WIDTH = VELS // VBLOCKS
SINK_RATE = 0.5
COURANT = 0.9
PACK = 4
EXT = 16
FIRST = 4
MESH = pl.DeviceIdType.MESH
BF16, F32 = jnp.bfloat16, jnp.float32


def grid_moments():
    centres = (2.0 * np.arange(VGRID) + 1.0 - VGRID) / VGRID
    second = float(np.sum(centres**2))
    fourth = float(np.sum(centres**4))
    number = float(VGRID)
    total = number**3
    cross = 3.0 * number * number * second
    quartic = 3.0 * number * number * fourth + 6.0 * number * second * second
    square = number * number * second
    return (total, cross, quartic, square)


def tables(cells):
    rows = np.full(cells + EXT, 10**6)
    rows[:cells] = np.arange(cells)
    rows[cells : cells + 4] = [-2, -1, cells, cells + 1]
    second = rows[None, :] - rows[:cells, None]
    second = np.where(rows[None, :] > 10**5, 9, second)
    cols = np.arange(cells + 2 * EXT)
    cols[cells : cells + EXT] = np.arange(EXT) % 4 - 4
    cols[cells + EXT :] = cells + np.arange(EXT) % 4
    first = cols[None, :] - rows[:, None]
    group = np.full((8, cells + 2 * EXT), -1)
    group[:, cells:] = np.arange(2 * EXT) % EXT // 4
    clean = lambda table: np.where(np.abs(table) <= 2, table, 9)
    return [t.astype(np.float32) for t in (clean(first), clean(second), group)]


def fixed_rows():
    column = np.arange(WIDTH)
    rows = np.zeros((8, WIDTH), np.float32)
    rows[0] = 2 * (column // VGRID % VGRID) + 1 - VGRID
    rows[1] = 2 * (column % VGRID) + 1 - VGRID
    return rows


def stencil(courant, table):
    a = jnp.abs(courant)
    u = (1.0 - a) * 0.5
    q = (1.0 - a * a) * (1.0 / 6.0)
    near = a * (1.0 - u + 3.0 * q)
    far = -a * q
    ahead = -a * (u - q)
    here = 1.0 - a * (1.0 - 2.0 * u + 3.0 * q)
    up = courant >= 0.0
    weights = {
        -2: jnp.where(up, far, 0.0),
        -1: jnp.where(up, near, ahead),
        0: here,
        1: jnp.where(up, ahead, near),
        2: jnp.where(up, 0.0, far),
    }
    full = jnp.zeros(table.shape, F32)
    for offset, weight in weights.items():
        full = jnp.where(table == offset, weight, full)
    high = full.astype(BF16)
    low = (full - high.astype(F32)).astype(BF16)
    return jnp.concatenate([high, low], axis=1)


def dot(a, b):
    return jnp.dot(a, b, preferred_element_type=F32)


def dot_t(a, b, **kw):
    return lax.dot_general(a, b, (((1,), (1,)), ((), ())), preferred_element_type=F32, **kw)


def kernel(
    n, owners, cells, scale,
    blocks_ref, coder_hbm, dens_hbm, left_ref, right_ref, first_ref, second_ref, group_ref, fixed_ref,
    inflow_ref, keep_ref, w_ref, bias_ref, rest_ref,
    out_hbm,
    basis_ref, energy_ref, coder_v, p_v, f_v, acc, eacc, send, recv, part, precv, gath, esend, erecv, bgath, mult, act_v,
    coder_sem, dens_sem, out_sem, s_send, s_recv, g_send, g_recv, e_send, e_recv, c_send, c_recv,
):
    me = lax.axis_index("vel")
    count = coder_v.shape[0]
    rows = cells + EXT
    latent = coder_v.shape[2]
    piece = latent // owners

    def coder_copy(b):
        return pltpu.make_async_copy(coder_hbm.at[b], coder_v.at[b], coder_sem.at[b])

    def columns(b):
        return pl.ds(pl.multiple_of(b * WIDTH, 128), WIDTH)

    def dens_copy(b):
        return pltpu.make_async_copy(dens_hbm.at[:, columns(b)], p_v.at[b], dens_sem.at[b])

    def out_copy(b):
        return pltpu.make_async_copy(p_v.at[b], out_hbm.at[:, columns(b)], out_sem.at[b])

    @pl.loop(0, count)
    def _(b):
        dens_copy(b).start()
        coder_copy(b).start()

    barrier = pltpu.get_barrier_semaphore()
    for d in range(1, n):
        pl.semaphore_signal(
            barrier, inc=1, device_id={"vel": lax.rem(me + d, n)}, device_id_type=MESH
        )
    pl.semaphore_wait(barrier, n - 1)

    def only(test, run):
        if n == owners:
            run()
        else:
            pl.when(test)(run)

    def energy_of(f, b):
        e = energy_ref[b]
        total = f[:, :128] * e[:, :128]
        for g in range(128, WIDTH, 128):
            total += f[:, g : g + 128] * e[:, g : g + 128]
        return total

    def exchange(step, size):
        col = jnp.sum(eacc[:size], axis=1, keepdims=True)
        eye = lax.broadcasted_iota(jnp.int32, (size, 128), 0) == lax.broadcasted_iota(
            jnp.int32, (size, 128), 1
        )
        row = jnp.sum(jnp.where(eye, col, 0.0), axis=0, keepdims=True)
        esend[step] = jnp.broadcast_to(row, (8, 128))
        for q in range(owners):
            value = acc[:size, q * piece : (q + 1) * piece]
            part[q, :size] = value
            if step:
                send[q, :size] = value.astype(BF16)

        def remote(src, dst, ss, rs, d):
            return pltpu.make_async_remote_copy(
                src_ref=src, dst_ref=dst, send_sem=ss, recv_sem=rs,
                device_id={"vel": lax.rem(me + d, n)}, device_id_type=MESH,
            )

        def scatter(d):
            to = lax.rem(me + d, n)
            if step == 0:
                src, dst = part.at[to], precv.at[d - 1]
            else:
                src, dst = send.at[to, pl.ds(0, size)], recv.at[d - 1, pl.ds(0, size)]
            return [remote(src, dst, s_send.at[step, d - 1], s_recv.at[step, d - 1], d)]

        def spread(d):
            made = [
                remote(
                    gath.at[step, me, pl.ds(0, size)], gath.at[step, me, pl.ds(0, size)],
                    g_send.at[step, d - 1], g_recv.at[step, me], d,
                )
            ]
            if step == 0:
                made.append(
                    remote(bgath.at[me], bgath.at[me], c_send.at[d - 1], c_recv.at[me], d)
                )
            return made

        def arrival(owner):
            made = [
                remote(
                    gath.at[step, owner, pl.ds(0, size)], gath.at[step, owner, pl.ds(0, size)],
                    g_send.at[step, 0], g_recv.at[step, owner], 1,
                )
            ]
            if step == 0:
                made.append(
                    remote(bgath.at[owner], bgath.at[owner], c_send.at[0], c_recv.at[owner], 1)
                )
            return made

        def tell(d):
            return remote(
                esend.at[step], erecv.at[step, d - 1], e_send.at[step, d - 1], e_recv.at[step, d - 1], d
            )

        for d in range(1, n):
            only(lax.rem(me + d, n) < owners, lambda d=d: [c.start() for c in scatter(d)] and None)
        for d in range(1, n):
            tell(d).start()

        def reduce():
            total = part[me, :size]
            for d in range(1, n):
                for c in scatter(d):
                    c.wait_recv()
                total += (recv[d - 1, :size] if step else precv[d - 1]).astype(F32)
            gath[step, me, :size] = total.astype(BF16)
            if step == 0:
                bgath[me] = total[cells:]
            for d in range(1, n):
                for c in spread(d):
                    c.start()

        only(me < owners, reduce)
        for d in range(1, n):
            only(lax.rem(me + d, n) < owners, lambda d=d: [c.wait_send() for c in scatter(d)] and None)
        for d in range(1, n):
            tell(d).wait()
        only(me < owners, lambda: [c.wait_send() for d in range(1, n) for c in spread(d)] and None)
        for d in range(1, n):
            owner = lax.rem(me + d, n)
            only(owner < owners, lambda owner=owner: [c.wait_recv() for c in arrival(owner)] and None)
        row = esend[step]
        for d in range(1, n):
            row += erecv[step, d - 1]
        return jnp.sum(jnp.where(eye, row[:1], 0.0), axis=1, keepdims=True)

    def latent_layer(step, size):
        energy_sum = exchange(step, size)
        encoded = jnp.concatenate([gath[step, q, :size] for q in range(owners)], axis=1)
        active = jnp.tanh(dot(encoded, w_ref[...]) + bias_ref[...]).astype(BF16)
        act_v[:size] = active
        base = jnp.concatenate([bgath[q] for q in range(owners)], axis=1)
        sums = scale * dot_t(active.astype(F32), base, precision=lax.Precision.HIGHEST)
        total, cross, quartic, square = grid_moments()
        sink = -SINK_RATE * (1.0 - rest_ref[:size] * rest_ref[:size]) * energy_sum
        grid = float(VGRID)
        m = [sums[:, FIRST + i : FIRST + i + 1] for i in range(6)]
        excess = (m[4] + m[5]) / (grid * grid) - sink
        determinant = total * quartic - cross * cross
        mass_mult = (quartic * m[0] - cross * excess) / determinant
        energy_mult = (total * excess - cross * m[0]) / determinant / (grid * grid)
        values = [mass_mult] + [m[i] / (square * grid * grid) for i in (1, 2, 3)] + [energy_mult] * 2
        lane = lax.broadcasted_iota(jnp.int32, (size, 2 * EXT), 1)
        full = jnp.zeros((size, 2 * EXT), F32)
        for i, value in enumerate(values):
            full = jnp.where(lane % EXT == FIRST + i, -value, full)
        high = full.astype(BF16).astype(F32)
        mult[:size] = jnp.where(lane < EXT, high, full - high).astype(BF16)

    def advanced(b, size):
        base = basis_ref[b]
        collision = dot_t(act_v[:size], coder_v[b])
        correction = dot(mult[:size], jnp.concatenate([base, base], axis=0))
        return (f_v[b, :size] + correction + scale * collision).astype(BF16)

    def courant(b):
        along = 2 * (blocks_ref[b] * WIDTH // (VGRID * VGRID)) + 1 - VGRID
        return along.astype(F32)

    def velocity_rows(b):
        nx = courant(b)
        ny = fixed_ref[:1] + (2 * (blocks_ref[b] * (WIDTH // VGRID) % VGRID)).astype(F32)
        nz = fixed_ref[1:2]
        kinetic = nx * nx + ny * ny + nz * nz
        upper = jnp.floor(kinetic * (1.0 / 64.0)) * 64.0
        energy_ref[b] = kinetic * (1.0 / (VGRID * VGRID))
        full = jnp.zeros((EXT, WIDTH), F32)
        for i, value in enumerate((1.0, nx, ny, nz, upper, kinetic - upper)):
            full = jnp.where(extra == FIRST + i, value, full)
        basis_ref[b] = full.astype(BF16)
        return full

    extra = lax.broadcasted_iota(jnp.int32, (EXT, WIDTH), 0)
    unit = math.gcd(count, 2)
    speed = COURANT / VGRID

    def coder_rows(start):
        return coder_v[pl.ds(start, unit)].reshape(unit * WIDTH, latent)

    def zero():
        acc[...] = jnp.zeros_like(acc)
        eacc[...] = jnp.zeros_like(eacc)

    zero()

    @pl.loop(0, count // unit)
    def _(g):
        parts = []
        for u in range(unit):
            b = g * unit + u
            dens_copy(b).wait()
            x = jnp.concatenate([p_v[b], left_ref[b // PACK], right_ref[b // PACK]], axis=0)
            group = group_ref[:1]
            mine = (group < 0.0) | (group == (b % PACK).astype(F32))
            weights = stencil(courant(b) * speed, jnp.where(mine, first_ref[...], 9.0))
            f = dot(weights, jnp.concatenate([x, x], axis=0))
            base = velocity_rows(b)
            f_v[b] = f
            eacc[...] += energy_of(f, b)
            tail = jnp.where(extra >= FIRST, base, f[cells:]).astype(BF16)
            parts.append(jnp.concatenate([f[:cells].astype(BF16), tail], axis=0))
        for u in range(unit):
            coder_copy(g * unit + u).wait()
        acc[...] += dot(jnp.concatenate(parts, axis=1), coder_rows(g * unit))

    latent_layer(0, rows)
    zero()

    @pl.loop(0, count // unit)
    def _(g):
        parts = []
        for u in range(unit):
            b = g * unit + u
            state = advanced(b, rows)
            edge = jnp.where(keep_ref[...] > 0.0, state[cells:].astype(F32), inflow_ref[b])
            x = jnp.concatenate([state[:cells], edge.astype(BF16)], axis=0)
            weights = stencil(courant(b) * speed, second_ref[...])
            f = dot(weights, jnp.concatenate([x, x], axis=0))
            f_v[b, :cells] = f
            eacc[:cells] += energy_of(f, b)
            parts.append(f.astype(BF16))
        acc[:cells] += dot(jnp.concatenate(parts, axis=1), coder_rows(g * unit))

    latent_layer(1, cells)

    @pl.loop(0, count // unit)
    def _(g):
        for u in range(unit):
            b = g * unit + u
            p_v[b] = advanced(b, cells)
        for u in range(unit):
            out_copy(g * unit + u).start()

    @pl.loop(0, count)
    def _(b):
        out_copy(b).wait()


def ring(value, step):
    count = lax.axis_size("cell") * lax.axis_size("sub")
    return lax.ppermute(value, ("cell", "sub"), [(i, (i + step) % count) for i in range(count)])


def body(density, coder, w_latent, b_latent, restitution, inflow, flags, blocks):
    cells, columns = density.shape
    latent = coder.shape[1]
    count = columns // WIDTH
    chunks = -(-count // PACK)
    n = lax.axis_size("vel")
    owners = min(n, latent // 128)
    rows = cells + EXT

    left = ring(density[-4:], 1)
    right = ring(density[:4], -1)
    rest_left = ring(restitution[-2:], 1)
    rest_right = ring(restitution[:2], -1)

    sub_count = lax.axis_size("sub")
    position = lax.axis_index("cell") * sub_count + lax.axis_index("sub")
    block_count = lax.axis_size("cell") * sub_count
    open_left = lax.dynamic_index_in_dim(flags, position, 0, keepdims=False) == 1
    open_right = (
        lax.dynamic_index_in_dim(flags, (position + 1) % block_count, 0, keepdims=False) == 1
    )

    first, second, group = tables(cells)

    def packed(ghosts, is_open):
        ghosts = jnp.where(is_open, ghosts, inflow.astype(BF16)[None])
        ghosts = ghosts.reshape(4, count, WIDTH).transpose(1, 0, 2)
        ghosts = jnp.pad(ghosts, ((0, chunks * PACK - count), (0, 0), (0, 0)))
        return ghosts.reshape(chunks, PACK * 4, WIDTH)

    rest = jnp.concatenate([restitution, rest_left, rest_right, jnp.zeros((EXT - 4,), F32)])
    side = jnp.arange(EXT)
    keep = jnp.where(side < 2, open_left, jnp.where(side < 4, open_right, True)).astype(F32)

    vmem = pl.BlockSpec(memory_space=pltpu.VMEM)
    hbm = pl.BlockSpec(memory_space=pl.ANY)
    dma = pltpu.SemaphoreType.DMA
    piece = latent // owners
    others = max(n - 1, 1)
    flops = 2 * columns * latent * (4 * rows) + 2 * columns * 512 * rows
    return pl.pallas_call(
        functools.partial(kernel, n, owners, cells, math.sqrt(VELS / latent)),
        out_shape=jax.ShapeDtypeStruct((cells, columns), BF16),
        in_specs=[pl.BlockSpec(memory_space=pltpu.SMEM), hbm, hbm] + [vmem] * 11,
        out_specs=hbm,
        scratch_shapes=[
            pltpu.VMEM((count, EXT, WIDTH), BF16),
            pltpu.VMEM((count, 1, WIDTH), F32),
            pltpu.VMEM((count, WIDTH, latent), BF16),
            pltpu.VMEM((count, cells, WIDTH), BF16),
            pltpu.VMEM((count, rows, WIDTH), F32),
            pltpu.VMEM((rows, latent), F32),
            pltpu.VMEM((rows, 128), F32),
            pltpu.VMEM((owners, rows, piece), BF16),
            pltpu.VMEM((others, rows, piece), BF16),
            pltpu.VMEM((owners, rows, piece), F32),
            pltpu.VMEM((others, rows, piece), F32),
            pltpu.VMEM((2, owners, rows, piece), BF16),
            pltpu.VMEM((2, 8, 128), F32),
            pltpu.VMEM((2, others, 8, 128), F32),
            pltpu.VMEM((owners, EXT, piece), F32),
            pltpu.VMEM((rows, 2 * EXT), BF16),
            pltpu.VMEM((rows, latent), BF16),
            dma((count,)), dma((count,)), dma((count,)),
            dma((2, others)), dma((2, others)), dma((2, others)), dma((2, owners)),
            dma((2, others)), dma((2, others)),
            dma((others,)), dma((owners,)),
        ],
        compiler_params=pltpu.CompilerParams(
            collective_id=0, has_side_effects=True, vmem_limit_bytes=60 * 1024 * 1024
        ),
        cost_estimate=pl.CostEstimate(
            flops=flops, bytes_accessed=2 * columns * (latent + 2 * cells), transcendentals=0
        ),
    )(
        blocks, coder.reshape(count, WIDTH, latent), density,
        packed(left, open_left), packed(right, open_right), first, second, group, fixed_rows(),
        inflow.reshape(count, 1, WIDTH), keep[:, None], w_latent, b_latent[None, :], rest[:, None],
    )


def solution(mesh):
    return jax.shard_map(
        body,
        mesh=mesh,
        in_specs=(
            P(("groups", "cell", "sub"), "vel"),
            P("vel", None),
            P(),
            P(),
            P(("groups", "cell", "sub")),
            P(("groups", "vel")),
            P("groups"),
            P(("groups", "vel")),
        ),
        out_specs=P(("groups", "cell", "sub"), "vel"),
        check_vma=False,
    )
```

```python
import functools
import math

import jax
import jax.numpy as jnp
import numpy as np
from jax import lax
from jax.experimental import pallas as pl
from jax.experimental.pallas import tpu as pltpu
from jax.sharding import PartitionSpec as P

VGRID = 48
VBLOCKS = 96
VELS = 110592
WIDTH = VELS // VBLOCKS
SINK_RATE = 0.5
COURANT = 0.9
PACK = 4
EXT = 16
FIRST = 4
MESH = pl.DeviceIdType.MESH
BF16, F32 = jnp.bfloat16, jnp.float32


def grid_moments():
    centres = (2.0 * np.arange(VGRID) + 1.0 - VGRID) / VGRID
    second = float(np.sum(centres**2))
    fourth = float(np.sum(centres**4))
    number = float(VGRID)
    total = number**3
    cross = 3.0 * number * number * second
    quartic = 3.0 * number * number * fourth + 6.0 * number * second * second
    square = number * number * second
    return (total, cross, quartic, square)


def tables(cells):
    rows = np.full(cells + EXT, 10**6)
    rows[:cells] = np.arange(cells)
    rows[cells : cells + 4] = [-2, -1, cells, cells + 1]
    second = rows[None, :] - rows[:cells, None]
    second = np.where(rows[None, :] > 10**5, 9, second)
    cols = np.arange(cells + 2 * EXT)
    cols[cells : cells + EXT] = np.arange(EXT) % 4 - 4
    cols[cells + EXT :] = cells + np.arange(EXT) % 4
    first = cols[None, :] - rows[:, None]
    group = np.full((8, cells + 2 * EXT), -1)
    group[:, cells:] = np.arange(2 * EXT) % EXT // 4
    clean = lambda table: np.where(np.abs(table) <= 2, table, 9)
    return [t.astype(np.float32) for t in (clean(first), clean(second), group)]


def fixed_rows():
    column = np.arange(WIDTH)
    rows = np.zeros((8, WIDTH), np.float32)
    rows[0] = 2 * (column // VGRID % VGRID) + 1 - VGRID
    rows[1] = 2 * (column % VGRID) + 1 - VGRID
    return rows


def stencil(courant, table):
    a = jnp.abs(courant)
    u = (1.0 - a) * 0.5
    q = (1.0 - a * a) * (1.0 / 6.0)
    near = a * (1.0 - u + 3.0 * q)
    far = -a * q
    ahead = -a * (u - q)
    here = 1.0 - a * (1.0 - 2.0 * u + 3.0 * q)
    up = courant >= 0.0
    weights = {
        -2: jnp.where(up, far, 0.0),
        -1: jnp.where(up, near, ahead),
        0: here,
        1: jnp.where(up, ahead, near),
        2: jnp.where(up, 0.0, far),
    }
    full = jnp.zeros(table.shape, F32)
    for offset, weight in weights.items():
        full = jnp.where(table == offset, weight, full)
    high = full.astype(BF16)
    low = (full - high.astype(F32)).astype(BF16)
    return jnp.concatenate([high, low], axis=1)


def dot(a, b):
    return jnp.dot(a, b, preferred_element_type=F32)


def dot_t(a, b, **kw):
    return lax.dot_general(a, b, (((1,), (1,)), ((), ())), preferred_element_type=F32, **kw)


def kernel(
    n, owners, cells, scale,
    blocks_ref, coder_hbm, dens_hbm, left_ref, right_ref, first_ref, second_ref, group_ref, fixed_ref,
    inflow_ref, keep_ref, w_ref, bias_ref, rest_ref,
    out_hbm,
    basis_ref, energy_ref, coder_v, p_v, f_v, acc, eacc, send, recv, part, precv, gath, esend, erecv, bgath, mult, act_v,
    coder_sem, dens_sem, out_sem, s_send, s_recv, g_send, g_recv, e_send, e_recv, c_send, c_recv,
):
    me = lax.axis_index("vel")
    count = coder_v.shape[0]
    rows = cells + EXT
    latent = coder_v.shape[2]
    piece = latent // owners

    def coder_copy(b):
        return pltpu.make_async_copy(coder_hbm.at[b], coder_v.at[b], coder_sem.at[b])

    def columns(b):
        return pl.ds(pl.multiple_of(b * WIDTH, 128), WIDTH)

    def dens_copy(b):
        return pltpu.make_async_copy(dens_hbm.at[:, columns(b)], p_v.at[b], dens_sem.at[b])

    def out_copy(b):
        return pltpu.make_async_copy(p_v.at[b], out_hbm.at[:, columns(b)], out_sem.at[b])

    @pl.loop(0, count)
    def _(b):
        dens_copy(b).start()
        coder_copy(b).start()

    barrier = pltpu.get_barrier_semaphore()
    for d in range(1, n):
        pl.semaphore_signal(
            barrier, inc=1, device_id={"vel": lax.rem(me + d, n)}, device_id_type=MESH
        )
    pl.semaphore_wait(barrier, n - 1)

    def only(test, run):
        if n == owners:
            run()
        else:
            pl.when(test)(run)

    def energy_of(f, b):
        e = energy_ref[b]
        total = f[:, :128] * e[:, :128]
        for g in range(128, WIDTH, 128):
            total += f[:, g : g + 128] * e[:, g : g + 128]
        return total

    def exchange(step, size):
        col = jnp.sum(eacc[:size], axis=1, keepdims=True)
        eye = lax.broadcasted_iota(jnp.int32, (size, 128), 0) == lax.broadcasted_iota(
            jnp.int32, (size, 128), 1
        )
        row = jnp.sum(jnp.where(eye, col, 0.0), axis=0, keepdims=True)
        esend[step] = jnp.broadcast_to(row, (8, 128))
        for q in range(owners):
            value = acc[:size, q * piece : (q + 1) * piece]
            part[q, :size] = value
            if step:
                send[q, :size] = value.astype(BF16)

        def remote(src, dst, ss, rs, d):
            return pltpu.make_async_remote_copy(
                src_ref=src, dst_ref=dst, send_sem=ss, recv_sem=rs,
                device_id={"vel": lax.rem(me + d, n)}, device_id_type=MESH,
            )

        def scatter(d):
            to = lax.rem(me + d, n)
            if step == 0:
                src, dst = part.at[to], precv.at[d - 1]
            else:
                src, dst = send.at[to, pl.ds(0, size)], recv.at[d - 1, pl.ds(0, size)]
            return [remote(src, dst, s_send.at[step, d - 1], s_recv.at[step, d - 1], d)]

        def spread(d):
            made = [
                remote(
                    gath.at[step, me, pl.ds(0, size)], gath.at[step, me, pl.ds(0, size)],
                    g_send.at[step, d - 1], g_recv.at[step, me], d,
                )
            ]
            if step == 0:
                made.append(
                    remote(bgath.at[me], bgath.at[me], c_send.at[d - 1], c_recv.at[me], d)
                )
            return made

        def arrival(owner):
            made = [
                remote(
                    gath.at[step, owner, pl.ds(0, size)], gath.at[step, owner, pl.ds(0, size)],
                    g_send.at[step, 0], g_recv.at[step, owner], 1,
                )
            ]
            if step == 0:
                made.append(
                    remote(bgath.at[owner], bgath.at[owner], c_send.at[0], c_recv.at[owner], 1)
                )
            return made

        def tell(d):
            return remote(
                esend.at[step], erecv.at[step, d - 1], e_send.at[step, d - 1], e_recv.at[step, d - 1], d
            )

        for d in range(1, n):
            only(lax.rem(me + d, n) < owners, lambda d=d: [c.start() for c in scatter(d)] and None)
        for d in range(1, n):
            tell(d).start()

        def reduce():
            total = part[me, :size]
            for d in range(1, n):
                for c in scatter(d):
                    c.wait_recv()
                total += (recv[d - 1, :size] if step else precv[d - 1]).astype(F32)
            gath[step, me, :size] = total.astype(BF16)
            if step == 0:
                bgath[me] = total[cells:]
            for d in range(1, n):
                for c in spread(d):
                    c.start()

        only(me < owners, reduce)
        for d in range(1, n):
            only(lax.rem(me + d, n) < owners, lambda d=d: [c.wait_send() for c in scatter(d)] and None)
        for d in range(1, n):
            tell(d).wait()
        only(me < owners, lambda: [c.wait_send() for d in range(1, n) for c in spread(d)] and None)
        for d in range(1, n):
            owner = lax.rem(me + d, n)
            only(owner < owners, lambda owner=owner: [c.wait_recv() for c in arrival(owner)] and None)
        row = esend[step]
        for d in range(1, n):
            row += erecv[step, d - 1]
        return jnp.sum(jnp.where(eye, row[:1], 0.0), axis=1, keepdims=True)

    def latent_layer(step, size):
        energy_sum = exchange(step, size)
        encoded = jnp.concatenate([gath[step, q, :size] for q in range(owners)], axis=1)
        active = jnp.tanh(dot(encoded, w_ref[...]) + bias_ref[...]).astype(BF16)
        act_v[:, :size] = active.astype(F32).T.astype(BF16)
        base = jnp.concatenate([bgath[q] for q in range(owners)], axis=1)
        sums = scale * dot_t(active.astype(F32), base, precision=lax.Precision.HIGHEST)
        total, cross, quartic, square = grid_moments()
        sink = -SINK_RATE * (1.0 - rest_ref[:size] * rest_ref[:size]) * energy_sum
        grid = float(VGRID)
        m = [sums[:, FIRST + i : FIRST + i + 1] for i in range(6)]
        excess = (m[4] + m[5]) / (grid * grid) - sink
        determinant = total * quartic - cross * cross
        mass_mult = (quartic * m[0] - cross * excess) / determinant
        energy_mult = (total * excess - cross * m[0]) / determinant / (grid * grid)
        values = [mass_mult] + [m[i] / (square * grid * grid) for i in (1, 2, 3)] + [energy_mult] * 2
        lane = lax.broadcasted_iota(jnp.int32, (size, 2 * EXT), 1)
        full = jnp.zeros((size, 2 * EXT), F32)
        for i, value in enumerate(values):
            full = jnp.where(lane % EXT == FIRST + i, -value, full)
        high = full.astype(BF16).astype(F32)
        mult[:size] = jnp.where(lane < EXT, high, full - high).astype(BF16)

    def advanced(b, size):
        base = basis_ref[b]
        collision = dot(coder_v[b], act_v[...]).T[:size]
        correction = dot(mult[:size], jnp.concatenate([base, base], axis=0))
        return (f_v[b, :size] + correction + scale * collision).astype(BF16)

    def courant(b):
        along = 2 * (blocks_ref[b] * WIDTH // (VGRID * VGRID)) + 1 - VGRID
        return along.astype(F32)

    def velocity_rows(b):
        nx = courant(b)
        ny = fixed_ref[:1] + (2 * (blocks_ref[b] * (WIDTH // VGRID) % VGRID)).astype(F32)
        nz = fixed_ref[1:2]
        kinetic = nx * nx + ny * ny + nz * nz
        upper = jnp.floor(kinetic * (1.0 / 64.0)) * 64.0
        energy_ref[b] = kinetic * (1.0 / (VGRID * VGRID))
        full = jnp.zeros((EXT, WIDTH), F32)
        for i, value in enumerate((1.0, nx, ny, nz, upper, kinetic - upper)):
            full = jnp.where(extra == FIRST + i, value, full)
        basis_ref[b] = full.astype(BF16)
        return full

    extra = lax.broadcasted_iota(jnp.int32, (EXT, WIDTH), 0)
    unit = math.gcd(count, 2)
    speed = COURANT / VGRID

    def coder_rows(start):
        return coder_v[pl.ds(start, unit)].reshape(unit * WIDTH, latent)

    act_v[...] = jnp.zeros_like(act_v)

    def zero():
        acc[...] = jnp.zeros_like(acc)
        eacc[...] = jnp.zeros_like(eacc)

    zero()

    @pl.loop(0, count // unit)
    def _(g):
        parts = []
        for u in range(unit):
            b = g * unit + u
            dens_copy(b).wait()
            x = jnp.concatenate([p_v[b], left_ref[b // PACK], right_ref[b // PACK]], axis=0)
            group = group_ref[:1]
            mine = (group < 0.0) | (group == (b % PACK).astype(F32))
            weights = stencil(courant(b) * speed, jnp.where(mine, first_ref[...], 9.0))
            f = dot(weights, jnp.concatenate([x, x], axis=0))
            base = velocity_rows(b)
            f_v[b] = f
            eacc[...] += energy_of(f, b)
            tail = jnp.where(extra >= FIRST, base, f[cells:]).astype(BF16)
            parts.append(jnp.concatenate([f[:cells].astype(BF16), tail], axis=0))
        for u in range(unit):
            coder_copy(g * unit + u).wait()
        acc[...] += dot(jnp.concatenate(parts, axis=1), coder_rows(g * unit))

    latent_layer(0, rows)
    zero()

    @pl.loop(0, count // unit)
    def _(g):
        parts = []
        for u in range(unit):
            b = g * unit + u
            state = advanced(b, rows)
            edge = jnp.where(keep_ref[...] > 0.0, state[cells:].astype(F32), inflow_ref[b])
            x = jnp.concatenate([state[:cells], edge.astype(BF16)], axis=0)
            weights = stencil(courant(b) * speed, second_ref[...])
            f = dot(weights, jnp.concatenate([x, x], axis=0))
            f_v[b, :cells] = f
            eacc[:cells] += energy_of(f, b)
            parts.append(f.astype(BF16))
        acc[:cells] += dot(jnp.concatenate(parts, axis=1), coder_rows(g * unit))

    latent_layer(1, cells)

    @pl.loop(0, count // unit)
    def _(g):
        for u in range(unit):
            b = g * unit + u
            p_v[b] = advanced(b, cells)
        for u in range(unit):
            out_copy(g * unit + u).start()

    @pl.loop(0, count)
    def _(b):
        out_copy(b).wait()


def ring(value, step):
    count = lax.axis_size("cell") * lax.axis_size("sub")
    return lax.ppermute(value, ("cell", "sub"), [(i, (i + step) % count) for i in range(count)])


def body(density, coder, w_latent, b_latent, restitution, inflow, flags, blocks):
    cells, columns = density.shape
    latent = coder.shape[1]
    count = columns // WIDTH
    chunks = -(-count // PACK)
    n = lax.axis_size("vel")
    owners = min(n, latent // 128)
    rows = cells + EXT

    left = ring(density[-4:], 1)
    right = ring(density[:4], -1)
    rest_left = ring(restitution[-2:], 1)
    rest_right = ring(restitution[:2], -1)

    sub_count = lax.axis_size("sub")
    position = lax.axis_index("cell") * sub_count + lax.axis_index("sub")
    block_count = lax.axis_size("cell") * sub_count
    open_left = lax.dynamic_index_in_dim(flags, position, 0, keepdims=False) == 1
    open_right = (
        lax.dynamic_index_in_dim(flags, (position + 1) % block_count, 0, keepdims=False) == 1
    )

    first, second, group = tables(cells)

    def packed(ghosts, is_open):
        ghosts = jnp.where(is_open, ghosts, inflow.astype(BF16)[None])
        ghosts = ghosts.reshape(4, count, WIDTH).transpose(1, 0, 2)
        ghosts = jnp.pad(ghosts, ((0, chunks * PACK - count), (0, 0), (0, 0)))
        return ghosts.reshape(chunks, PACK * 4, WIDTH)

    rest = jnp.concatenate([restitution, rest_left, rest_right, jnp.zeros((EXT - 4,), F32)])
    side = jnp.arange(EXT)
    keep = jnp.where(side < 2, open_left, jnp.where(side < 4, open_right, True)).astype(F32)

    vmem = pl.BlockSpec(memory_space=pltpu.VMEM)
    hbm = pl.BlockSpec(memory_space=pl.ANY)
    dma = pltpu.SemaphoreType.DMA
    piece = latent // owners
    others = max(n - 1, 1)
    flops = 2 * columns * latent * (4 * rows) + 2 * columns * 512 * rows
    return pl.pallas_call(
        functools.partial(kernel, n, owners, cells, math.sqrt(VELS / latent)),
        out_shape=jax.ShapeDtypeStruct((cells, columns), BF16),
        in_specs=[pl.BlockSpec(memory_space=pltpu.SMEM), hbm, hbm] + [vmem] * 11,
        out_specs=hbm,
        scratch_shapes=[
            pltpu.VMEM((count, EXT, WIDTH), BF16),
            pltpu.VMEM((count, 1, WIDTH), F32),
            pltpu.VMEM((count, WIDTH, latent), BF16),
            pltpu.VMEM((count, cells, WIDTH), BF16),
            pltpu.VMEM((count, rows, WIDTH), F32),
            pltpu.VMEM((rows, latent), F32),
            pltpu.VMEM((rows, 128), F32),
            pltpu.VMEM((owners, rows, piece), BF16),
            pltpu.VMEM((others, rows, piece), BF16),
            pltpu.VMEM((owners, rows, piece), F32),
            pltpu.VMEM((others, rows, piece), F32),
            pltpu.VMEM((2, owners, rows, piece), BF16),
            pltpu.VMEM((2, 8, 128), F32),
            pltpu.VMEM((2, others, 8, 128), F32),
            pltpu.VMEM((owners, EXT, piece), F32),
            pltpu.VMEM((rows, 2 * EXT), BF16),
            pltpu.VMEM((latent, -(-rows // 128) * 128), BF16),
            dma((count,)), dma((count,)), dma((count,)),
            dma((2, others)), dma((2, others)), dma((2, others)), dma((2, owners)),
            dma((2, others)), dma((2, others)),
            dma((others,)), dma((owners,)),
        ],
        compiler_params=pltpu.CompilerParams(
            collective_id=0, has_side_effects=True, vmem_limit_bytes=60 * 1024 * 1024
        ),
        cost_estimate=pl.CostEstimate(
            flops=flops, bytes_accessed=2 * columns * (latent + 2 * cells), transcendentals=0
        ),
    )(
        blocks, coder.reshape(count, WIDTH, latent), density,
        packed(left, open_left), packed(right, open_right), first, second, group, fixed_rows(),
        inflow.reshape(count, 1, WIDTH), keep[:, None], w_latent, b_latent[None, :], rest[:, None],
    )


def solution(mesh):
    return jax.shard_map(
        body,
        mesh=mesh,
        in_specs=(
            P(("groups", "cell", "sub"), "vel"),
            P("vel", None),
            P(),
            P(),
            P(("groups", "cell", "sub")),
            P(("groups", "vel")),
            P("groups"),
            P(("groups", "vel")),
        ),
        out_specs=P(("groups", "cell", "sub"), "vel"),
        check_vma=False,
    )
```

```python
import functools
import math

import jax
import jax.numpy as jnp
import numpy as np
from jax import lax
from jax.experimental import pallas as pl
from jax.experimental.pallas import tpu as pltpu
from jax.sharding import PartitionSpec as P

VGRID = 48
VBLOCKS = 96
VELS = 110592
WIDTH = VELS // VBLOCKS
SINK_RATE = 0.5
COURANT = 0.9
PACK = 4
EXT = 16
FIRST = 4
MESH = pl.DeviceIdType.MESH
BF16, F32 = jnp.bfloat16, jnp.float32


def grid_moments():
    centres = (2.0 * np.arange(VGRID) + 1.0 - VGRID) / VGRID
    second = float(np.sum(centres**2))
    fourth = float(np.sum(centres**4))
    number = float(VGRID)
    total = number**3
    cross = 3.0 * number * number * second
    quartic = 3.0 * number * number * fourth + 6.0 * number * second * second
    square = number * number * second
    return (total, cross, quartic, square)


def tables(cells):
    rows = np.full(cells + EXT, 10**6)
    rows[:cells] = np.arange(cells)
    rows[cells : cells + 4] = [-2, -1, cells, cells + 1]
    second = rows[None, :] - rows[:cells, None]
    second = np.where(rows[None, :] > 10**5, 9, second)
    cols = np.arange(cells + 2 * EXT)
    cols[cells : cells + EXT] = np.arange(EXT) % 4 - 4
    cols[cells + EXT :] = cells + np.arange(EXT) % 4
    first = cols[None, :] - rows[:, None]
    group = np.full((8, cells + 2 * EXT), -1)
    group[:, cells:] = np.arange(2 * EXT) % EXT // 4
    clean = lambda table: np.where(np.abs(table) <= 2, table, 9)
    return [t.astype(np.float32) for t in (clean(first), clean(second), group)]


def fixed_rows():
    column = np.arange(WIDTH)
    rows = np.zeros((8, WIDTH), np.float32)
    rows[0] = 2 * (column // VGRID % VGRID) + 1 - VGRID
    rows[1] = 2 * (column % VGRID) + 1 - VGRID
    return rows


def stencil(courant, table):
    a = jnp.abs(courant)
    u = (1.0 - a) * 0.5
    q = (1.0 - a * a) * (1.0 / 6.0)
    near = a * (1.0 - u + 3.0 * q)
    far = -a * q
    ahead = -a * (u - q)
    here = 1.0 - a * (1.0 - 2.0 * u + 3.0 * q)
    up = courant >= 0.0
    weights = {
        -2: jnp.where(up, far, 0.0),
        -1: jnp.where(up, near, ahead),
        0: here,
        1: jnp.where(up, ahead, near),
        2: jnp.where(up, 0.0, far),
    }
    full = jnp.zeros(table.shape, F32)
    for offset, weight in weights.items():
        full = jnp.where(table == offset, weight, full)
    high = full.astype(BF16)
    low = (full - high.astype(F32)).astype(BF16)
    return jnp.concatenate([high, low], axis=1)


def dot(a, b):
    return jnp.dot(a, b, preferred_element_type=F32)


def dot_t(a, b, **kw):
    return lax.dot_general(a, b, (((1,), (1,)), ((), ())), preferred_element_type=F32, **kw)


def kernel(
    n, owners, cells, scale,
    blocks_ref, flags_ref, coder_hbm, dens_hbm, first_ref, second_ref, group_ref, fixed_ref,
    inflow_ref, w_ref, bias_ref, rest_ref,
    out_hbm,
    to_right, to_left, left_ref, right_ref, rest_left, rest_right, h_send, h_recv, r_send, r_recv,
    basis_ref, energy_ref, coder_v, p_v, f_v, acc, eacc, send, recv, part, precv, gath, esend, erecv, bgath, mult, act_v,
    coder_sem, dens_sem, out_sem, s_send, s_recv, g_send, g_recv, e_send, e_recv, c_send, c_recv,
):
    me = lax.axis_index("vel")
    subs = lax.axis_size("sub")
    ring = lax.axis_size("cell") * subs
    place = lax.axis_index("cell") * subs + lax.axis_index("sub")
    next_place, last_place = lax.rem(place + 1, ring), lax.rem(place + ring - 1, ring)
    on_right = {"cell": next_place // subs, "sub": lax.rem(next_place, subs)}
    on_left = {"cell": last_place // subs, "sub": lax.rem(last_place, subs)}
    count = coder_v.shape[0]
    rows = cells + EXT
    latent = coder_v.shape[2]
    piece = latent // owners

    def coder_copy(b):
        return pltpu.make_async_copy(coder_hbm.at[b], coder_v.at[b], coder_sem.at[b])

    def columns(b):
        return pl.ds(pl.multiple_of(b * WIDTH, 128), WIDTH)

    def dens_copy(b):
        return pltpu.make_async_copy(dens_hbm.at[:, columns(b)], p_v.at[b], dens_sem.at[b])

    def out_copy(b):
        return pltpu.make_async_copy(p_v.at[b], out_hbm.at[:, columns(b)], out_sem.at[b])

    @pl.loop(0, count)
    def _(b):
        dens_copy(b).start()

    @pl.loop(0, count)
    def _(b):
        coder_copy(b).start()

    barrier = pltpu.get_barrier_semaphore()
    for d in range(1, n):
        pl.semaphore_signal(
            barrier, inc=1, device_id={"vel": lax.rem(me + d, n)}, device_id_type=MESH
        )
    for neighbour in (on_left, on_right):
        pl.semaphore_signal(barrier, inc=1, device_id=neighbour, device_id_type=MESH)
    pl.semaphore_wait(barrier, n + 1)

    pack = min(PACK, count)
    chunks = count // pack

    def halo_copies(c):
        return [
            pltpu.make_async_remote_copy(
                src_ref=src.at[c], dst_ref=dst.at[c], send_sem=h_send.at[i, c],
                recv_sem=h_recv.at[i, c], device_id=to, device_id_type=MESH,
            )
            for i, (src, dst, to) in enumerate(
                ((to_right, left_ref, on_right), (to_left, right_ref, on_left))
            )
        ]

    def rest_copies():
        return [
            pltpu.make_async_remote_copy(
                src_ref=rest_ref, dst_ref=dst, send_sem=r_send.at[i],
                recv_sem=r_recv.at[i], device_id=to, device_id_type=MESH,
            )
            for i, (dst, to) in enumerate(((rest_left, on_right), (rest_right, on_left)))
        ]

    for copy in rest_copies():
        copy.start()

    pick_row = lax.broadcasted_iota(jnp.int32, (4 * PACK, 16 * pack), 0)
    pick_col = lax.broadcasted_iota(jnp.int32, (4 * PACK, 16 * pack), 1)
    pick = (pick_row // 4) * 16 + pick_row % 4
    pick_head = jnp.where(pick_col == pick, 1.0, 0.0).astype(BF16)
    pick_tail = jnp.where(pick_col == pick + 12, 1.0, 0.0).astype(BF16)

    @pl.loop(0, chunks)
    def _(c):
        for u in range(pack):
            dens_copy(c * pack + u).wait()
        heads = jnp.concatenate([p_v[c * pack + u, :16] for u in range(pack)], axis=0)
        tails = jnp.concatenate([p_v[c * pack + u, cells - 16 :] for u in range(pack)], axis=0)
        to_left[c] = dot(pick_head, heads).astype(BF16)
        to_right[c] = dot(pick_tail, tails).astype(BF16)
        for copy in halo_copies(c):
            copy.start()

    open_left = flags_ref[place].astype(F32)
    open_right = flags_ref[next_place].astype(F32)

    def rest_column(size):
        eye = lax.broadcasted_iota(jnp.int32, (size, 128), 0) == lax.broadcasted_iota(
            jnp.int32, (size, 128), 1
        )
        lane = lax.broadcasted_iota(jnp.int32, (1, 128), 1)
        row = jnp.where(lane < cells, rest_ref[:1], 0.0)
        row = jnp.where((lane >= cells) & (lane < cells + 2), rest_left[1:2], row)
        row = jnp.where((lane >= cells + 2) & (lane < cells + 4), rest_right[2:3], row)
        return jnp.sum(jnp.where(eye, row, 0.0), axis=1, keepdims=True)

    def only(test, run):
        if n == owners:
            run()
        else:
            pl.when(test)(run)

    def energy_of(f, b):
        e = energy_ref[b]
        total = f[:, :128] * e[:, :128]
        for g in range(128, WIDTH, 128):
            total += f[:, g : g + 128] * e[:, g : g + 128]
        return total

    def exchange(step, size):
        col = jnp.sum(eacc[:size], axis=1, keepdims=True)
        eye = lax.broadcasted_iota(jnp.int32, (size, 128), 0) == lax.broadcasted_iota(
            jnp.int32, (size, 128), 1
        )
        row = jnp.sum(jnp.where(eye, col, 0.0), axis=0, keepdims=True)
        esend[step] = jnp.broadcast_to(row, (8, 128))
        for q in range(owners):
            value = acc[:size, q * piece : (q + 1) * piece]
            part[q, :size] = value
            if step:
                send[q, :size] = value.astype(BF16)

        def remote(src, dst, ss, rs, d):
            return pltpu.make_async_remote_copy(
                src_ref=src, dst_ref=dst, send_sem=ss, recv_sem=rs,
                device_id={"vel": lax.rem(me + d, n)}, device_id_type=MESH,
            )

        def scatter(d):
            to = lax.rem(me + d, n)
            if step == 0:
                src, dst = part.at[to], precv.at[d - 1]
            else:
                src, dst = send.at[to, pl.ds(0, size)], recv.at[d - 1, pl.ds(0, size)]
            return [remote(src, dst, s_send.at[step, d - 1], s_recv.at[step, d - 1], d)]

        def spread(d):
            made = [
                remote(
                    gath.at[step, me, pl.ds(0, size)], gath.at[step, me, pl.ds(0, size)],
                    g_send.at[step, d - 1], g_recv.at[step, me], d,
                )
            ]
            if step == 0:
                made.append(
                    remote(bgath.at[me], bgath.at[me], c_send.at[d - 1], c_recv.at[me], d)
                )
            return made

        def arrival(owner):
            made = [
                remote(
                    gath.at[step, owner, pl.ds(0, size)], gath.at[step, owner, pl.ds(0, size)],
                    g_send.at[step, 0], g_recv.at[step, owner], 1,
                )
            ]
            if step == 0:
                made.append(
                    remote(bgath.at[owner], bgath.at[owner], c_send.at[0], c_recv.at[owner], 1)
                )
            return made

        def tell(d):
            return remote(
                esend.at[step], erecv.at[step, d - 1], e_send.at[step, d - 1], e_recv.at[step, d - 1], d
            )

        for d in range(1, n):
            only(lax.rem(me + d, n) < owners, lambda d=d: [c.start() for c in scatter(d)] and None)
        for d in range(1, n):
            tell(d).start()

        def reduce():
            total = part[me, :size]
            for d in range(1, n):
                for c in scatter(d):
                    c.wait_recv()
                total += (recv[d - 1, :size] if step else precv[d - 1]).astype(F32)
            gath[step, me, :size] = total.astype(BF16)
            if step == 0:
                bgath[me] = total[cells:]
            for d in range(1, n):
                for c in spread(d):
                    c.start()

        only(me < owners, reduce)
        for d in range(1, n):
            only(lax.rem(me + d, n) < owners, lambda d=d: [c.wait_send() for c in scatter(d)] and None)
        for d in range(1, n):
            tell(d).wait()
        only(me < owners, lambda: [c.wait_send() for d in range(1, n) for c in spread(d)] and None)
        for d in range(1, n):
            owner = lax.rem(me + d, n)
            only(owner < owners, lambda owner=owner: [c.wait_recv() for c in arrival(owner)] and None)
        row = esend[step]
        for d in range(1, n):
            row += erecv[step, d - 1]
        return jnp.sum(jnp.where(eye, row[:1], 0.0), axis=1, keepdims=True)

    def latent_layer(step, size):
        energy_sum = exchange(step, size)
        encoded = jnp.concatenate([gath[step, q, :size] for q in range(owners)], axis=1)
        active = jnp.tanh(dot(encoded, w_ref[...]) + bias_ref[...]).astype(BF16)
        act_v[:size] = active
        base = jnp.concatenate([bgath[q] for q in range(owners)], axis=1)
        sums = scale * dot_t(active.astype(F32), base, precision=lax.Precision.HIGHEST)
        total, cross, quartic, square = grid_moments()
        if step == 0:
            for copy in rest_copies():
                copy.wait()
        rest = rest_column(size)
        sink = -SINK_RATE * (1.0 - rest * rest) * energy_sum
        grid = float(VGRID)
        m = [sums[:, FIRST + i : FIRST + i + 1] for i in range(6)]
        excess = (m[4] + m[5]) / (grid * grid) - sink
        determinant = total * quartic - cross * cross
        mass_mult = (quartic * m[0] - cross * excess) / determinant
        energy_mult = (total * excess - cross * m[0]) / determinant / (grid * grid)
        values = [mass_mult] + [m[i] / (square * grid * grid) for i in (1, 2, 3)] + [energy_mult] * 2
        lane = lax.broadcasted_iota(jnp.int32, (size, 2 * EXT), 1)
        full = jnp.zeros((size, 2 * EXT), F32)
        for i, value in enumerate(values):
            full = jnp.where(lane % EXT == FIRST + i, -value, full)
        high = full.astype(BF16).astype(F32)
        mult[:size] = jnp.where(lane < EXT, high, full - high).astype(BF16)

    def advanced(b, size):
        base = basis_ref[b]
        collision = dot_t(act_v[:size], coder_v[b])
        correction = dot(mult[:size], jnp.concatenate([base, base], axis=0))
        return (f_v[b, :size] + correction + scale * collision).astype(BF16)

    def courant(b):
        along = 2 * (blocks_ref[b] * WIDTH // (VGRID * VGRID)) + 1 - VGRID
        return along.astype(F32)

    def velocity_rows(b):
        nx = courant(b)
        ny = fixed_ref[:1] + (2 * (blocks_ref[b] * (WIDTH // VGRID) % VGRID)).astype(F32)
        nz = fixed_ref[1:2]
        kinetic = nx * nx + ny * ny + nz * nz
        upper = jnp.floor(kinetic * (1.0 / 64.0)) * 64.0
        energy_ref[b] = kinetic * (1.0 / (VGRID * VGRID))
        full = jnp.zeros((EXT, WIDTH), F32)
        for i, value in enumerate((1.0, nx, ny, nz, upper, kinetic - upper)):
            full = jnp.where(extra == FIRST + i, value, full)
        basis_ref[b] = full.astype(BF16)
        return full

    extra = lax.broadcasted_iota(jnp.int32, (EXT, WIDTH), 0)
    unit = math.gcd(pack, 2)
    speed = COURANT / VGRID

    keep = jnp.where(extra < 2, open_left, jnp.where(extra < 4, open_right, 1.0))

    def coder_rows(start):
        return coder_v[pl.ds(start, unit)].reshape(unit * WIDTH, latent)

    def zero():
        acc[...] = jnp.zeros_like(acc)
        eacc[...] = jnp.zeros_like(eacc)

    zero()

    @pl.loop(0, chunks)
    def _(c):
        for copy in halo_copies(c):
            copy.wait()
        parts = []
        for u in range(pack):
            b = c * pack + u
            inflow = jnp.broadcast_to(inflow_ref[b], (4 * PACK, WIDTH))
            ghosts = [
                jnp.where(jnp.full((4 * PACK, WIDTH), is_open) > 0.0, held[c].astype(F32), inflow)
                for held, is_open in ((left_ref, open_left), (right_ref, open_right))
            ]
            x = jnp.concatenate([p_v[b]] + [g.astype(BF16) for g in ghosts], axis=0)
            group = group_ref[:1]
            mine = (group < 0.0) | (group == float(u))
            weights = stencil(courant(b) * speed, jnp.where(mine, first_ref[...], 9.0))
            f = dot(weights, jnp.concatenate([x, x], axis=0))
            base = velocity_rows(b)
            f_v[b] = f
            eacc[...] += energy_of(f, b)
            tail = jnp.where(extra >= FIRST, base, f[cells:]).astype(BF16)
            parts.append(jnp.concatenate([f[:cells].astype(BF16), tail], axis=0))
            if len(parts) == unit:
                start = b + 1 - unit
                for v in range(unit):
                    coder_copy(start + v).wait()
                acc[...] += dot(jnp.concatenate(parts, axis=1), coder_rows(start))
                parts = []

    latent_layer(0, rows)
    zero()

    @pl.loop(0, count // unit)
    def _(g):
        parts = []
        for u in range(unit):
            b = g * unit + u
            state = advanced(b, rows)
            inflow = jnp.broadcast_to(inflow_ref[b], (EXT, WIDTH))
            edge = jnp.where(keep > 0.0, state[cells:].astype(F32), inflow)
            x = jnp.concatenate([state[:cells], edge.astype(BF16)], axis=0)
            weights = stencil(courant(b) * speed, second_ref[...])
            f = dot(weights, jnp.concatenate([x, x], axis=0))
            f_v[b, :cells] = f
            eacc[:cells] += energy_of(f, b)
            parts.append(f.astype(BF16))
        acc[:cells] += dot(jnp.concatenate(parts, axis=1), coder_rows(g * unit))

    latent_layer(1, cells)

    @pl.loop(0, count // unit)
    def _(g):
        for u in range(unit):
            b = g * unit + u
            p_v[b] = advanced(b, cells)
        for u in range(unit):
            out_copy(g * unit + u).start()

    @pl.loop(0, count)
    def _(b):
        out_copy(b).wait()


def body(density, coder, w_latent, b_latent, restitution, inflow, flags, blocks):
    cells, columns = density.shape
    latent = coder.shape[1]
    count = columns // WIDTH
    chunks = -(-count // PACK)
    ghost = pltpu.VMEM((chunks, 4 * PACK, WIDTH), BF16)
    n = lax.axis_size("vel")
    owners = min(n, latent // 128)
    rows = cells + EXT

    first, second, group = tables(cells)

    rest = jnp.zeros((8, 128), F32).at[0, :cells].set(restitution)
    rest = rest.at[1, cells : cells + 2].set(restitution[-2:])
    rest = rest.at[2, cells + 2 : cells + 4].set(restitution[:2])

    vmem = pl.BlockSpec(memory_space=pltpu.VMEM)
    smem = pl.BlockSpec(memory_space=pltpu.SMEM)
    hbm = pl.BlockSpec(memory_space=pl.ANY)
    dma = pltpu.SemaphoreType.DMA
    piece = latent // owners
    others = max(n - 1, 1)
    flops = 2 * columns * latent * (4 * rows) + 2 * columns * 512 * rows
    return pl.pallas_call(
        functools.partial(kernel, n, owners, cells, math.sqrt(VELS / latent)),
        out_shape=jax.ShapeDtypeStruct((cells, columns), BF16),
        in_specs=[smem, smem, hbm, hbm] + [vmem] * 8,
        out_specs=hbm,
        scratch_shapes=[
            ghost, ghost, ghost, ghost, pltpu.VMEM((8, 128), F32), pltpu.VMEM((8, 128), F32),
            dma((2, chunks)), dma((2, chunks)), dma((2,)), dma((2,)),
            pltpu.VMEM((count, EXT, WIDTH), BF16),
            pltpu.VMEM((count, 1, WIDTH), F32),
            pltpu.VMEM((count, WIDTH, latent), BF16),
            pltpu.VMEM((count, cells, WIDTH), BF16),
            pltpu.VMEM((count, rows, WIDTH), F32),
            pltpu.VMEM((rows, latent), F32),
            pltpu.VMEM((rows, 128), F32),
            pltpu.VMEM((owners, rows, piece), BF16),
            pltpu.VMEM((others, rows, piece), BF16),
            pltpu.VMEM((owners, rows, piece), F32),
            pltpu.VMEM((others, rows, piece), F32),
            pltpu.VMEM((2, owners, rows, piece), BF16),
            pltpu.VMEM((2, 8, 128), F32),
            pltpu.VMEM((2, others, 8, 128), F32),
            pltpu.VMEM((owners, EXT, piece), F32),
            pltpu.VMEM((rows, 2 * EXT), BF16),
            pltpu.VMEM((rows, latent), BF16),
            dma((count,)), dma((count,)), dma((count,)),
            dma((2, others)), dma((2, others)), dma((2, others)), dma((2, owners)),
            dma((2, others)), dma((2, others)),
            dma((others,)), dma((owners,)),
        ],
        compiler_params=pltpu.CompilerParams(
            collective_id=0, has_side_effects=True, vmem_limit_bytes=60 * 1024 * 1024
        ),
        cost_estimate=pl.CostEstimate(
            flops=flops, bytes_accessed=2 * columns * (latent + 2 * cells), transcendentals=0
        ),
    )(
        blocks, flags, coder.reshape(count, WIDTH, latent), density, first, second, group, fixed_rows(),
        inflow.reshape(count, 1, WIDTH), w_latent, b_latent[None, :], rest,
    )


def solution(mesh):
    return jax.shard_map(
        body,
        mesh=mesh,
        in_specs=(
            P(("groups", "cell", "sub"), "vel"),
            P("vel", None),
            P(),
            P(),
            P(("groups", "cell", "sub")),
            P(("groups", "vel")),
            P("groups"),
            P(("groups", "vel")),
        ),
        out_specs=P(("groups", "cell", "sub"), "vel"),
        check_vma=False,
    )
```

```python
import functools
import math

import jax
import jax.numpy as jnp
import numpy as np
from jax import lax
from jax.experimental import pallas as pl
from jax.experimental.pallas import tpu as pltpu
from jax.sharding import PartitionSpec as P

VGRID = 48
VBLOCKS = 96
VELS = 110592
WIDTH = VELS // VBLOCKS
SINK_RATE = 0.5
COURANT = 0.9
PACK = 4
EXT = 16
FIRST = 4
MESH = pl.DeviceIdType.MESH
BF16, F32 = jnp.bfloat16, jnp.float32


def grid_moments():
    centres = (2.0 * np.arange(VGRID) + 1.0 - VGRID) / VGRID
    second = float(np.sum(centres**2))
    fourth = float(np.sum(centres**4))
    number = float(VGRID)
    total = number**3
    cross = 3.0 * number * number * second
    quartic = 3.0 * number * number * fourth + 6.0 * number * second * second
    square = number * number * second
    return (total, cross, quartic, square)


def tables(cells):
    rows = np.full(cells + EXT, 10**6)
    rows[:cells] = np.arange(cells)
    rows[cells : cells + 4] = [-2, -1, cells, cells + 1]
    second = rows[None, :] - rows[:cells, None]
    second = np.where(rows[None, :] > 10**5, 9, second)
    cols = np.arange(cells + 2 * EXT)
    cols[cells : cells + EXT] = np.arange(EXT) % 4 - 4
    cols[cells + EXT :] = cells + np.arange(EXT) % 4
    first = cols[None, :] - rows[:, None]
    group = np.full((8, cells + 2 * EXT), -1)
    group[:, cells:] = np.arange(2 * EXT) % EXT // 4
    clean = lambda table: np.where(np.abs(table) <= 2, table, 9)
    return [t.astype(np.float32) for t in (clean(first), clean(second), group)]


def fixed_rows():
    column = np.arange(WIDTH)
    rows = np.zeros((8, WIDTH), np.float32)
    rows[0] = 2 * (column // VGRID % VGRID) + 1 - VGRID
    rows[1] = 2 * (column % VGRID) + 1 - VGRID
    return rows


def stencil(courant, table):
    a = jnp.abs(courant)
    u = (1.0 - a) * 0.5
    q = (1.0 - a * a) * (1.0 / 6.0)
    near = a * (1.0 - u + 3.0 * q)
    far = -a * q
    ahead = -a * (u - q)
    here = 1.0 - a * (1.0 - 2.0 * u + 3.0 * q)
    up = courant >= 0.0
    weights = {
        -2: jnp.where(up, far, 0.0),
        -1: jnp.where(up, near, ahead),
        0: here,
        1: jnp.where(up, ahead, near),
        2: jnp.where(up, 0.0, far),
    }
    full = jnp.zeros(table.shape, F32)
    for offset, weight in weights.items():
        full = jnp.where(table == offset, weight, full)
    high = full.astype(BF16)
    low = (full - high.astype(F32)).astype(BF16)
    return jnp.concatenate([high, low], axis=1)


def dot(a, b):
    return jnp.dot(a, b, preferred_element_type=F32)


def dot_t(a, b, **kw):
    return lax.dot_general(a, b, (((1,), (1,)), ((), ())), preferred_element_type=F32, **kw)


def kernel(
    n, owners, cells, scale,
    blocks_ref, flags_ref, coder_hbm, dens_hbm, first_ref, second_ref, group_ref, fixed_ref,
    inflow_ref, w_ref, bias_ref, rest_ref,
    out_hbm,
    to_right, to_left, left_ref, right_ref, rest_left, rest_right, h_send, h_recv, r_send, r_recv,
    basis_ref, energy_ref, coder_v, p_v, f_v, acc, eacc, send, recv, part, precv, gath, esend, erecv, bgath, act_v,
    coder_sem, dens_sem, out_sem, s_send, s_recv, g_send, g_recv, e_send, e_recv, c_send, c_recv,
):
    me = lax.axis_index("vel")
    subs = lax.axis_size("sub")
    ring = lax.axis_size("cell") * subs
    place = lax.axis_index("cell") * subs + lax.axis_index("sub")
    next_place, last_place = lax.rem(place + 1, ring), lax.rem(place + ring - 1, ring)
    on_right = {"cell": next_place // subs, "sub": lax.rem(next_place, subs)}
    on_left = {"cell": last_place // subs, "sub": lax.rem(last_place, subs)}
    count = coder_v.shape[0]
    rows = cells + EXT
    latent = coder_v.shape[2]
    piece = latent // owners

    def coder_copy(b):
        return pltpu.make_async_copy(coder_hbm.at[b], coder_v.at[b], coder_sem.at[b])

    def columns(b):
        return pl.ds(pl.multiple_of(b * WIDTH, 128), WIDTH)

    def dens_copy(b):
        return pltpu.make_async_copy(dens_hbm.at[:, columns(b)], p_v.at[b], dens_sem.at[b])

    def out_copy(b):
        return pltpu.make_async_copy(p_v.at[b], out_hbm.at[:, columns(b)], out_sem.at[b])

    @pl.loop(0, count)
    def _(b):
        dens_copy(b).start()

    @pl.loop(0, count)
    def _(b):
        coder_copy(b).start()

    barrier = pltpu.get_barrier_semaphore()
    for d in range(1, n):
        pl.semaphore_signal(
            barrier, inc=1, device_id={"vel": lax.rem(me + d, n)}, device_id_type=MESH
        )
    for neighbour in (on_left, on_right):
        pl.semaphore_signal(barrier, inc=1, device_id=neighbour, device_id_type=MESH)
    pl.semaphore_wait(barrier, n + 1)

    pack = min(PACK, count)
    chunks = count // pack

    def halo_copies(c):
        return [
            pltpu.make_async_remote_copy(
                src_ref=src.at[c], dst_ref=dst.at[c], send_sem=h_send.at[i, c],
                recv_sem=h_recv.at[i, c], device_id=to, device_id_type=MESH,
            )
            for i, (src, dst, to) in enumerate(
                ((to_right, left_ref, on_right), (to_left, right_ref, on_left))
            )
        ]

    def rest_copies():
        return [
            pltpu.make_async_remote_copy(
                src_ref=rest_ref, dst_ref=dst, send_sem=r_send.at[i],
                recv_sem=r_recv.at[i], device_id=to, device_id_type=MESH,
            )
            for i, (dst, to) in enumerate(((rest_left, on_right), (rest_right, on_left)))
        ]

    for copy in rest_copies():
        copy.start()

    pick_row = lax.broadcasted_iota(jnp.int32, (4 * PACK, 16 * pack), 0)
    pick_col = lax.broadcasted_iota(jnp.int32, (4 * PACK, 16 * pack), 1)
    pick = (pick_row // 4) * 16 + pick_row % 4
    pick_head = jnp.where(pick_col == pick, 1.0, 0.0).astype(BF16)
    pick_tail = jnp.where(pick_col == pick + 12, 1.0, 0.0).astype(BF16)

    @pl.loop(0, chunks)
    def _(c):
        for u in range(pack):
            dens_copy(c * pack + u).wait()
        heads = jnp.concatenate([p_v[c * pack + u, :16] for u in range(pack)], axis=0)
        tails = jnp.concatenate([p_v[c * pack + u, cells - 16 :] for u in range(pack)], axis=0)
        to_left[c] = dot(pick_head, heads).astype(BF16)
        to_right[c] = dot(pick_tail, tails).astype(BF16)
        for copy in halo_copies(c):
            copy.start()

    open_left = flags_ref[place].astype(F32)
    open_right = flags_ref[next_place].astype(F32)

    def rest_column(size):
        eye = lax.broadcasted_iota(jnp.int32, (size, 128), 0) == lax.broadcasted_iota(
            jnp.int32, (size, 128), 1
        )
        lane = lax.broadcasted_iota(jnp.int32, (1, 128), 1)
        row = jnp.where(lane < cells, rest_ref[:1], 0.0)
        row = jnp.where((lane >= cells) & (lane < cells + 2), rest_left[1:2], row)
        row = jnp.where((lane >= cells + 2) & (lane < cells + 4), rest_right[2:3], row)
        return jnp.sum(jnp.where(eye, row, 0.0), axis=1, keepdims=True)

    def only(test, run):
        if n == owners:
            run()
        else:
            pl.when(test)(run)

    def energy_of(f, b):
        e = energy_ref[b]
        total = f[:, :128] * e[:, :128]
        for g in range(128, WIDTH, 128):
            total += f[:, g : g + 128] * e[:, g : g + 128]
        return total

    def exchange(step, size, between):
        col = jnp.sum(eacc[:size], axis=1, keepdims=True)
        eye = lax.broadcasted_iota(jnp.int32, (size, 128), 0) == lax.broadcasted_iota(
            jnp.int32, (size, 128), 1
        )
        row = jnp.sum(jnp.where(eye, col, 0.0), axis=0, keepdims=True)
        esend[step] = jnp.broadcast_to(row, (8, 128))
        for q in range(owners):
            value = acc[:size, q * piece : (q + 1) * piece]
            part[q, :size] = value
            if step:
                send[q, :size] = value.astype(BF16)

        def remote(src, dst, ss, rs, d):
            return pltpu.make_async_remote_copy(
                src_ref=src, dst_ref=dst, send_sem=ss, recv_sem=rs,
                device_id={"vel": lax.rem(me + d, n)}, device_id_type=MESH,
            )

        def scatter(d):
            to = lax.rem(me + d, n)
            if step == 0:
                src, dst = part.at[to], precv.at[d - 1]
            else:
                src, dst = send.at[to, pl.ds(0, size)], recv.at[d - 1, pl.ds(0, size)]
            return [remote(src, dst, s_send.at[step, d - 1], s_recv.at[step, d - 1], d)]

        def spread(d):
            made = [
                remote(
                    gath.at[step, me, pl.ds(0, size)], gath.at[step, me, pl.ds(0, size)],
                    g_send.at[step, d - 1], g_recv.at[step, me], d,
                )
            ]
            if step == 0:
                made.append(
                    remote(bgath.at[me], bgath.at[me], c_send.at[d - 1], c_recv.at[me], d)
                )
            return made

        def arrival(owner):
            made = [
                remote(
                    gath.at[step, owner, pl.ds(0, size)], gath.at[step, owner, pl.ds(0, size)],
                    g_send.at[step, 0], g_recv.at[step, owner], 1,
                )
            ]
            if step == 0:
                made.append(
                    remote(bgath.at[owner], bgath.at[owner], c_send.at[0], c_recv.at[owner], 1)
                )
            return made

        def tell(d):
            return remote(
                esend.at[step], erecv.at[step, d - 1], e_send.at[step, d - 1], e_recv.at[step, d - 1], d
            )

        for d in range(1, n):
            only(lax.rem(me + d, n) < owners, lambda d=d: [c.start() for c in scatter(d)] and None)
        for d in range(1, n):
            tell(d).start()
        between()

        def reduce():
            total = part[me, :size]
            for d in range(1, n):
                for c in scatter(d):
                    c.wait_recv()
                total += (recv[d - 1, :size] if step else precv[d - 1]).astype(F32)
            gath[step, me, :size] = total.astype(BF16)
            if step == 0:
                bgath[me] = total[cells:]
            for d in range(1, n):
                for c in spread(d):
                    c.start()

        only(me < owners, reduce)
        for d in range(1, n):
            only(lax.rem(me + d, n) < owners, lambda d=d: [c.wait_send() for c in scatter(d)] and None)
        for d in range(1, n):
            tell(d).wait()
        only(me < owners, lambda: [c.wait_send() for d in range(1, n) for c in spread(d)] and None)
        for d in range(1, n):
            owner = lax.rem(me + d, n)
            only(owner < owners, lambda owner=owner: [c.wait_recv() for c in arrival(owner)] and None)
        row = esend[step]
        for d in range(1, n):
            row += erecv[step, d - 1]
        return jnp.sum(jnp.where(eye, row[:1], 0.0), axis=1, keepdims=True)

    def latent_layer(step, size, between):
        energy_sum = exchange(step, size, between)
        encoded = jnp.concatenate([gath[step, q, :size] for q in range(owners)], axis=1)
        active = jnp.tanh(dot(encoded, w_ref[...]) + bias_ref[...]).astype(BF16)
        act_v[:size, :latent] = active
        base = jnp.concatenate([bgath[q] for q in range(owners)], axis=1)
        sums = scale * dot_t(active.astype(F32), base, precision=lax.Precision.HIGHEST)
        total, cross, quartic, square = grid_moments()
        if step == 0:
            for copy in rest_copies():
                copy.wait()
        rest = rest_column(size)
        sink = -SINK_RATE * (1.0 - rest * rest) * energy_sum
        grid = float(VGRID)
        m = [sums[:, FIRST + i : FIRST + i + 1] for i in range(6)]
        excess = (m[4] + m[5]) / (grid * grid) - sink
        determinant = total * quartic - cross * cross
        mass_mult = (quartic * m[0] - cross * excess) / determinant
        energy_mult = (total * excess - cross * m[0]) / determinant / (grid * grid)
        values = [mass_mult] + [m[i] / (square * grid * grid) for i in (1, 2, 3)] + [energy_mult] * 2
        lane = lax.broadcasted_iota(jnp.int32, (size, 128), 1)
        full = jnp.zeros((size, 128), F32)
        for i, value in enumerate(values):
            full = jnp.where((lane % EXT == FIRST + i) & (lane < 2 * EXT), -value, full)
        high = full.astype(BF16).astype(F32)
        act_v[:size, latent:] = jnp.where(lane < EXT, high, full - high).astype(BF16)

    def advanced(b, size, active, mult):
        base = basis_ref[b]
        collision = dot_t(active, coder_v[b])
        correction = dot(mult, jnp.concatenate([base] * (mult.shape[1] // EXT), axis=0))
        return f_v[b, :size] + correction + scale * collision

    def courant(b):
        along = 2 * (blocks_ref[b] * WIDTH // (VGRID * VGRID)) + 1 - VGRID
        return along.astype(F32)

    def velocity_rows(b):
        nx = courant(b)
        ny = fixed_ref[:1] + (2 * (blocks_ref[b] * (WIDTH // VGRID) % VGRID)).astype(F32)
        nz = fixed_ref[1:2]
        kinetic = nx * nx + ny * ny + nz * nz
        upper = jnp.floor(kinetic * (1.0 / 64.0)) * 64.0
        energy_ref[b] = kinetic * (1.0 / (VGRID * VGRID))
        full = jnp.zeros((EXT, WIDTH), F32)
        for i, value in enumerate((1.0, nx, ny, nz, upper, kinetic - upper)):
            full = jnp.where(extra == FIRST + i, value, full)
        basis_ref[b] = full.astype(BF16)
        return full

    extra = lax.broadcasted_iota(jnp.int32, (EXT, WIDTH), 0)
    unit = math.gcd(pack, 2)
    speed = COURANT / VGRID

    keep = jnp.where(extra < 2, open_left, jnp.where(extra < 4, open_right, 1.0))

    def coder_rows(start):
        return coder_v[pl.ds(start, unit)].reshape(unit * WIDTH, latent)

    def zero():
        acc[...] = jnp.zeros_like(acc)
        eacc[...] = jnp.zeros_like(eacc)

    zero()

    @pl.loop(0, chunks)
    def _(c):
        for copy in halo_copies(c):
            copy.wait()
        parts = []
        for u in range(pack):
            b = c * pack + u
            inflow = jnp.broadcast_to(inflow_ref[b], (4 * PACK, WIDTH))
            ghosts = [
                jnp.where(jnp.full((4 * PACK, WIDTH), is_open) > 0.0, held[c].astype(F32), inflow)
                for held, is_open in ((left_ref, open_left), (right_ref, open_right))
            ]
            x = jnp.concatenate([p_v[b]] + [g.astype(BF16) for g in ghosts], axis=0)
            group = group_ref[:1]
            mine = (group < 0.0) | (group == float(u))
            weights = stencil(courant(b) * speed, jnp.where(mine, first_ref[...], 9.0))
            f = dot(weights, jnp.concatenate([x, x], axis=0))
            base = velocity_rows(b)
            f_v[b] = f
            eacc[...] += energy_of(f, b)
            tail = jnp.where(extra >= FIRST, base, f[cells:]).astype(BF16)
            parts.append(jnp.concatenate([f[:cells].astype(BF16), tail], axis=0))
            if len(parts) == unit:
                start = b + 1 - unit
                for v in range(unit):
                    coder_copy(start + v).wait()
                acc[...] += dot(jnp.concatenate(parts, axis=1), coder_rows(start))
                parts = []

    def transported():
        @pl.loop(0, count // unit)
        def _(g):
            for u in range(unit):
                b = g * unit + u
                f = f_v[b]
                inflow = jnp.broadcast_to(inflow_ref[b], (EXT, WIDTH))
                edge = jnp.where(keep > 0.0, f[cells:], inflow)
                x = jnp.concatenate([f[:cells].astype(BF16), edge.astype(BF16)], axis=0)
                weights = stencil(courant(b) * speed, second_ref[...])
                f_v[b, :cells] = dot(weights, jnp.concatenate([x, x], axis=0))

    latent_layer(0, rows, transported)
    zero()
    column = lax.broadcasted_iota(jnp.int32, (cells, rows), 1) - cells
    shut = ((column >= 0) & (column < 2) & (jnp.full((cells, rows), open_left) == 0.0)) | (
        (column >= 2) & (jnp.full((cells, rows), open_right) == 0.0)
    )
    inner = jnp.where(shut, 9.0, second_ref[...])
    lanes = lax.broadcasted_iota(jnp.int32, (cells, 128), 1)

    @pl.loop(0, chunks)
    def _(c):
        parts = []
        for u in range(pack):
            b = c * pack + u
            held = act_v[...]
            moved = dot(stencil(courant(b) * speed, inner), jnp.concatenate([held, held], axis=0))
            mult = moved[:, latent:]
            high = mult.astype(BF16).astype(F32)
            low = pltpu.roll(mult - high, 2 * EXT, axis=1)
            mult = jnp.where(lanes < 2 * EXT, high, low).astype(BF16)[:, : 4 * EXT]
            f = advanced(b, cells, moved[:, :latent].astype(BF16), mult)
            f_v[b, :cells] = f
            eacc[:cells] += energy_of(f, b)
            parts.append(f.astype(BF16))
            if len(parts) == unit:
                acc[:cells] += dot(jnp.concatenate(parts, axis=1), coder_rows(b + 1 - unit))
                parts = []

    latent_layer(1, cells, lambda: None)

    @pl.loop(0, chunks)
    def _(c):
        active = act_v[:cells, :latent]
        mult = act_v[:cells, latent : latent + 2 * EXT]
        for u in range(pack):
            b = c * pack + u
            p_v[b] = advanced(b, cells, active, mult).astype(BF16)
            out_copy(b).start()

    @pl.loop(0, count)
    def _(b):
        out_copy(b).wait()


def body(density, coder, w_latent, b_latent, restitution, inflow, flags, blocks):
    cells, columns = density.shape
    latent = coder.shape[1]
    count = columns // WIDTH
    chunks = -(-count // PACK)
    ghost = pltpu.VMEM((chunks, 4 * PACK, WIDTH), BF16)
    n = lax.axis_size("vel")
    owners = min(n, latent // 128)
    rows = cells + EXT

    first, second, group = tables(cells)

    rest = jnp.zeros((8, 128), F32).at[0, :cells].set(restitution)
    rest = rest.at[1, cells : cells + 2].set(restitution[-2:])
    rest = rest.at[2, cells + 2 : cells + 4].set(restitution[:2])

    vmem = pl.BlockSpec(memory_space=pltpu.VMEM)
    smem = pl.BlockSpec(memory_space=pltpu.SMEM)
    hbm = pl.BlockSpec(memory_space=pl.ANY)
    dma = pltpu.SemaphoreType.DMA
    piece = latent // owners
    others = max(n - 1, 1)
    flops = 2 * columns * latent * (4 * rows) + 2 * columns * 512 * rows
    return pl.pallas_call(
        functools.partial(kernel, n, owners, cells, math.sqrt(VELS / latent)),
        out_shape=jax.ShapeDtypeStruct((cells, columns), BF16),
        in_specs=[smem, smem, hbm, hbm] + [vmem] * 8,
        out_specs=hbm,
        scratch_shapes=[
            ghost, ghost, ghost, ghost, pltpu.VMEM((8, 128), F32), pltpu.VMEM((8, 128), F32),
            dma((2, chunks)), dma((2, chunks)), dma((2,)), dma((2,)),
            pltpu.VMEM((count, EXT, WIDTH), BF16),
            pltpu.VMEM((count, 1, WIDTH), F32),
            pltpu.VMEM((count, WIDTH, latent), BF16),
            pltpu.VMEM((count, cells, WIDTH), BF16),
            pltpu.VMEM((count, rows, WIDTH), F32),
            pltpu.VMEM((rows, latent), F32),
            pltpu.VMEM((rows, 128), F32),
            pltpu.VMEM((owners, rows, piece), BF16),
            pltpu.VMEM((others, rows, piece), BF16),
            pltpu.VMEM((owners, rows, piece), F32),
            pltpu.VMEM((others, rows, piece), F32),
            pltpu.VMEM((2, owners, rows, piece), BF16),
            pltpu.VMEM((2, 8, 128), F32),
            pltpu.VMEM((2, others, 8, 128), F32),
            pltpu.VMEM((owners, EXT, piece), F32),
            pltpu.VMEM((rows, latent + 128), BF16),
            dma((count,)), dma((count,)), dma((count,)),
            dma((2, others)), dma((2, others)), dma((2, others)), dma((2, owners)),
            dma((2, others)), dma((2, others)),
            dma((others,)), dma((owners,)),
        ],
        compiler_params=pltpu.CompilerParams(
            collective_id=0, has_side_effects=True, vmem_limit_bytes=60 * 1024 * 1024
        ),
        cost_estimate=pl.CostEstimate(
            flops=flops, bytes_accessed=2 * columns * (latent + 2 * cells), transcendentals=0
        ),
    )(
        blocks, flags, coder.reshape(count, WIDTH, latent), density, first, second, group, fixed_rows(),
        inflow.reshape(count, 1, WIDTH), w_latent, b_latent[None, :], rest,
    )


def solution(mesh):
    return jax.shard_map(
        body,
        mesh=mesh,
        in_specs=(
            P(("groups", "cell", "sub"), "vel"),
            P("vel", None),
            P(),
            P(),
            P(("groups", "cell", "sub")),
            P(("groups", "vel")),
            P("groups"),
            P(("groups", "vel")),
        ),
        out_specs=P(("groups", "cell", "sub"), "vel"),
        check_vma=False,
    )
```
